256 devices in a mesh: shard: 16 (over x, z_hi, core), rep: 16 (over y, z_lo).
Axes of the slice: x: 4, y: 4, z: 8 (z_hi: 2, z_lo: 4; z = z_hi * 4 + z_lo), core: 2. Of those that a mesh axis runs over, the one named last changes fastest.
Arguments:
- grads: bfloat16 [16, 16, 2097152], P('shard', 'rep'), may hold values from -5000 to 5000
- momentum_codes: int32 [2097152], P(('shard', 'rep')), may hold values from -127 to 127
- variance_codes: int32 [2097152], P(('shard', 'rep')), may hold values from 16 to 255
- momentum_scale: float32 [1280], P(('shard', 'rep')), may hold values from 0.5 to 4, as said below
- variance_scale: float32 [1280], P(('shard', 'rep')), may hold values from 1 to 4, as said below
- master: float32 [2097152], P(('shard', 'rep')), may hold values from -2.5 to 2.5
- step: int32 [1], replicated, may hold values from 1 to 19
Outputs:
- new_master: float32 [2097152], P(('shard', 'rep'))
- weights: bfloat16 [2097152], P('shard')
- update: float32 [2097152], P(('shard', 'rep'))
- momentum_norm: float32 [2097152], P(('shard', 'rep'))
- variance_norm: float32 [2097152], P(('shard', 'rep'))
- momentum_absmax: float32 [1280], P(('shard', 'rep'))
- variance_absmax: float32 [1280], P(('shard', 'rep'))
The draws below stay inside these ranges and needn't reach their ends.
Inputs may be any that keep to these rules, and one draw needn't show every extreme that they name: `momentum_scale`: A block touched by two neighbouring devices has the same value in both devices' slots. `variance_scale`: A block touched by two neighbouring devices has the same value in both devices' slots.
All inputs are finite; a program needn't handle non-finite values.
Results may differ from the reference program's by a relative error of at most 0.0004.
Values may be sent and summed in bfloat16 or wider, within the bound.
A program may use at most 64 MiB of HBM per device.

```python
import math
import jax
import jax.numpy as jnp
from jax import lax

BLOCK = 2048
FULL_BLOCKS = 4
OWN = 8192
SLOTS = 5
PARAMS = 2097152
N_SHARD = 16
N_REP = 16
DEVICES = 256


def slot_blocks():
    owner = jnp.arange(DEVICES, dtype=jnp.int32)[:, None]
    slot = jnp.arange(SLOTS, dtype=jnp.int32)[None, :]
    return (owner * FULL_BLOCKS + slot).reshape(-1).astype(jnp.int32)


def draw_scale(key, low, high):
    nblocks = PARAMS // BLOCK + 1
    values = jnp.exp(jax.random.uniform(key, (nblocks,), jnp.float32, math.log(low), math.log(high)))
    return values[slot_blocks()]


def draw_momentum_scale(key, part):
    return draw_scale(jax.random.fold_in(key, 11), 0.5, 4.0)


def draw_variance_scale(key, part):
    return draw_scale(jax.random.fold_in(key, 23), 1.0, 4.0)


def plant_codes(key, low, high, peak, upper, signed):
    nblocks = PARAMS // BLOCK + 1
    half_len = BLOCK // 2
    key_base, key_place, key_sign = jax.random.split(key, 3)
    base = jax.random.randint(key_base, (PARAMS,), low, high, dtype=jnp.int32)
    entry = jnp.arange(PARAMS, dtype=jnp.int32)
    block = (entry + half_len) // BLOCK
    within = (entry + half_len) % BLOCK
    place = jax.random.randint(key_place, (nblocks,), 0, half_len, dtype=jnp.int32)
    if upper:
        place = place + half_len
    chosen = within == place[block]
    if signed:
        signs = jax.random.randint(key_sign, (nblocks,), 0, 2, dtype=jnp.int32) * 2 - 1
        signs = signs.at[0].set(1).at[1].set(-1)
        planted = peak * signs[block]
    else:
        planted = jnp.full((PARAMS,), peak, jnp.int32)
    return jnp.where(chosen, planted, base).astype(jnp.int32)


def draw_momentum_codes(key, part):
    return plant_codes(jax.random.fold_in(key, 41), -63, 64, 127, True, True)


def draw_variance_codes(key, part):
    return plant_codes(jax.random.fold_in(key, 43), 16, 129, 255, False, False)


def draw_grads(key, part):
    keys = jax.random.split(jax.random.fold_in(key, 37), 9)
    nblocks = PARAMS // BLOCK
    position = jnp.arange(PARAMS, dtype=jnp.float32) / float(PARAMS)
    roughness = jnp.repeat(jnp.exp(jax.random.uniform(keys[0], (nblocks,), jnp.float32, 0.0, math.log(10.0))), BLOCK)
    device_scale = jnp.exp(jax.random.uniform(keys[1], (N_SHARD, N_REP, 1), jnp.float32, 0.0, math.log(3.0)))
    noise = jnp.clip(jax.random.normal(keys[2], (N_SHARD, N_REP, PARAMS), jnp.float32), -4.0, 4.0)
    perm_a = jax.random.permutation(keys[3], N_SHARD).astype(jnp.int32)
    perm_b = jax.random.permutation(keys[4], N_REP).astype(jnp.int32)
    partner = perm_a[:, None] * N_REP + perm_b[None, :]
    owner = jnp.arange(PARAMS, dtype=jnp.int32) // OWN
    heavy = (owner[None, None, :] == partner[:, :, None]).astype(jnp.float32)
    spike = 1.0 + 11.0 * heavy
    trend = jnp.power(3.0, position) * roughness
    quarter = BLOCK // 4
    odd_step = 2 * jax.random.randint(keys[6], (nblocks,), 0, max(quarter // 2, 1), dtype=jnp.int32) + 1
    region = jax.random.randint(keys[7], (nblocks,), 0, 2, dtype=jnp.int32)
    offset = quarter + region * 2 * quarter + odd_step
    sign_flip = (jax.random.randint(keys[8], (nblocks,), 0, 2, dtype=jnp.int32) * 2 - 1).astype(jnp.float32)
    entry = jnp.arange(PARAMS, dtype=jnp.int32)
    group_of = entry // BLOCK
    within = entry % BLOCK
    planted = (within == offset[group_of]).astype(jnp.float32) * sign_flip[group_of]
    spread_sq = 3.64 * float(DEVICES + 143)
    values = noise * device_scale * spike * trend
    height = math.sqrt(float(BLOCK) * spread_sq) / float(DEVICES)
    values = values + (height * planted * trend)[None, None, :]
    return values.astype(jnp.bfloat16)


def level_of(stream_key, extent, pieces, low, top_value):
    def one(axis_at, blocks):
        heights = jax.random.uniform(jax.random.fold_in(jax.random.fold_in(stream_key, 6), axis_at), (blocks,), jnp.float32, low / len(pieces), top_value / len(pieces))
        return jnp.repeat(jnp.exp(heights), extent[axis_at] // blocks).reshape((-1,) + (1,) * (len(extent) - axis_at - 1))

    gain = one(*pieces[0])
    for cut in pieces[1:]:
        gain = gain * one(*cut)
    return gain


def gaussian(key, shape, deviation, reach, cuts=(), kind=jnp.bfloat16):
    array = deviation * jax.random.normal(key, shape, jnp.float32)
    if cuts:
        array = array * level_of(key, shape, cuts, -0.22, 0.18)
    return jnp.clip(array, -reach, reach).astype(kind)


def setup_inputs(seed: int = 0) -> dict:
    key_of = jax.random.split(jax.random.key(seed), 8)
    grads = draw_grads(jax.random.fold_in(key_of[7], 71), 0)
    momentum_codes = draw_momentum_codes(jax.random.fold_in(key_of[7], 71), 0)
    variance_codes = draw_variance_codes(jax.random.fold_in(key_of[7], 71), 0)
    momentum_scale = draw_momentum_scale(jax.random.fold_in(key_of[7], 71), 0)
    variance_scale = draw_variance_scale(jax.random.fold_in(key_of[7], 71), 0)
    master = gaussian(key_of[5], (PARAMS,), 0.5, 2.5, ((0, 256),), jnp.float32)
    step = jax.random.randint(key_of[6], (1,), 1, 20).astype(jnp.int32)
    return {"grads": grads, "momentum_codes": momentum_codes, "variance_codes": variance_codes, "momentum_scale": momentum_scale, "variance_scale": variance_scale, "master": master, "step": step}


def slot_index():
    entry = jnp.arange(PARAMS, dtype=jnp.int32)
    owner = entry // OWN
    local = entry % OWN
    slot = (local + BLOCK // 2) // BLOCK
    return (owner * SLOTS + slot).astype(jnp.int32)

def block_of_slot():
    owner = jnp.arange(DEVICES, dtype=jnp.int32)[:, None]
    slot = jnp.arange(SLOTS, dtype=jnp.int32)[None, :]
    return (owner * FULL_BLOCKS + slot).reshape(-1).astype(jnp.int32)

def reference(grads, momentum_codes, variance_codes, momentum_scale, variance_scale, master, step):
    half = BLOCK // 2
    gsum = lax.optimization_barrier(jnp.sum(grads.astype(jnp.float32), axis=(0, 1)))
    norm_sq = jnp.sum(gsum * gsum)
    clip_factor = jnp.minimum(1.0, float(PARAMS) ** 0.5 / (jnp.sqrt(norm_sq) + 1e-06))
    scaled = gsum * clip_factor
    index = slot_index()
    m_old = momentum_codes.astype(jnp.float32) / 127.0 * momentum_scale[index]
    v_old = variance_codes.astype(jnp.float32) / 255.0 * variance_scale[index]
    momentum = 0.9 * m_old + 0.1 * scaled
    variance = 0.95 * v_old + 0.05 * scaled * scaled
    count = step[0].astype(jnp.float32)
    first_fix = 1.0 - jnp.power(jnp.float32(0.9), count)
    second_fix = 1.0 - jnp.power(jnp.float32(0.95), count)
    update = momentum / first_fix / (jnp.sqrt(variance / second_fix) + 1e-08)
    new_master = master * (1.0 - 0.0001 * 0.1) - 0.0001 * update
    weights = new_master.astype(jnp.bfloat16)
    nblocks = PARAMS // BLOCK + 1
    m_pad = jnp.pad(jnp.abs(momentum), (half, half))
    v_pad = jnp.pad(jnp.abs(variance), (half, half))
    m_block = lax.optimization_barrier(jnp.max(m_pad.reshape(nblocks, BLOCK), axis=1))
    v_block = lax.optimization_barrier(jnp.max(v_pad.reshape(nblocks, BLOCK), axis=1))
    m_elem = jnp.repeat(m_block, BLOCK)[half:half + PARAMS]
    v_elem = jnp.repeat(v_block, BLOCK)[half:half + PARAMS]
    momentum_norm = momentum / (m_elem + 1e-06)
    variance_norm = variance / (v_elem + 1e-06)
    slots = block_of_slot()
    return (new_master, weights, update, momentum_norm, variance_norm, m_block[slots], v_block[slots])
```

```python
import functools
import math

import jax
import jax.numpy as jnp
from jax import lax
from jax.experimental import pallas as pl
from jax.experimental.pallas import tpu as pltpu
from jax.sharding import PartitionSpec as P

MESH = pl.DeviceIdType.MESH
F32 = jnp.float32
BF16 = jnp.bfloat16

NX, NY, NZ = 4, 4, 8
ROWS = 64
PART_ROWS = (24, 24, 16)
RA, RB, RC = PART_ROWS
TOTAL = float(NX * NY * NZ * 2 * ROWS * 128)
GROUP = 131072
GROUP_ROWS = GROUP // 128

X_OFFSETS = (2, 1, 3, 0)
XY_PEERS = [(dx, dy) for dx in range(NX) for dy in range(NY) if dx or dy]
ZC_PEERS = [(dz, dc) for dz in range(NZ) for dc in range(2) if dz or dc]
REP_PEERS = [(dy, dl) for dy in range(4) for dl in range(4) if dy or dl]


def ring_sends(n):
    order = []
    for step in range(n // 2):
        order.append((1, n // 2 - step))
        if n // 2 - 1 - step >= 1:
            order.append((0, n // 2 - 1 - step))
    return order


def device(x, y, z, c):
    return ((x * 2 + lax.div(z, 4)) * 2 + c, y * 4 + lax.rem(z, 4))


def add_into(dst, src, rows, tile):
    def body(i, carry):
        at = pl.ds(pl.multiple_of(i * tile, tile), tile)
        dst[at, :] = dst[at, :] + src[at, :]
        return carry

    lax.fori_loop(0, rows // tile, body, 0)


def kernel(
    g_ref, mcode_ref, vcode_ref, master_ref, mscale_ref, vscale_ref, step_ref,
    new_ref, w_ref, up_ref, mn_ref, vn_ref, am_ref, av_ref,
    raw, pack, got, sa, sb, sc, ra, rb, rc, a2, b2, c2, a3, b3, c3,
    gs, old, n1, n2, n1r, n2r,
    load_sem, core_sem, ring_a, ring_b, ring_c, two_sem, three_a, three_b, three_c,
    edge_sem, norm1_sem, norm2_sem, out_sem,
):
    s, r = lax.axis_index("shard"), lax.axis_index("rep")
    x, c = lax.div(s, 4), lax.rem(s, 2)
    y, zl = lax.div(r, 4), lax.rem(r, 4)
    zh = lax.rem(lax.div(s, 2), 2)
    z = zh * 4 + zl
    o = s * 16 + r

    def rel(dx=0, dy=0, dz=0, dc=0):
        return device(
            lax.rem(x + dx + NX, NX), lax.rem(y + dy + NY, NY), lax.rem(z + dz + NZ, NZ), lax.rem(c + dc, 2)
        )

    def in_rep(dy, dl):
        return (s, lax.rem(y + dy, 4) * 4 + lax.rem(zl + dl, 4))

    def flat(step):
        to = lax.rem(o + step + 256, 256)
        return (lax.div(to, 16), lax.rem(to, 16))

    def remote(src, dst, sems, index, to):
        return pltpu.make_async_remote_copy(
            src_ref=src, dst_ref=dst, send_sem=sems.at[(0,) + index], recv_sem=sems.at[(1,) + index],
            device_id=to, device_id_type=MESH,
        )

    started = []

    def send(src, dst, sems, index, to):
        copy = remote(src, dst, sems, index, to)
        copy.start()
        started.append(copy)
        return copy

    loads = []
    for i in range(8):
        group = lax.rem(x + X_OFFSETS[i // 2], NX) * 2 + i % 2
        for own in (0, 1):
            core = c if own else 1 - c
            at = pl.multiple_of((group * 2 + core) * GROUP, GROUP)
            load = pltpu.make_async_copy(
                g_ref.at[0, :, pl.ds(at, GROUP)], raw.at[:, pl.ds((2 * i + own) * GROUP, GROUP)], load_sem.at[2 * i + own]
            )
            load.start()
            loads.append(load)

    barrier = pltpu.get_barrier_semaphore()
    peers = [rel(dx=dx, dy=dy) for dx, dy in XY_PEERS] + [rel(dz=dz, dc=dc) for dz, dc in ZC_PEERS]
    peers += [in_rep(dy, dl) for dy, dl in REP_PEERS] + [flat(1), flat(-1)]
    for peer in peers:
        pl.semaphore_signal(barrier, inc=1, device_id=peer, device_id_type=MESH)

    for j in range(5):
        low, high = max(16 * j - 8, 0), min(16 * j + 8, ROWS)
        old[0, 8 + low : 8 + high, :] = mcode_ref[low:high, :].astype(F32) / 127.0 * mscale_ref[j]
        old[1, 8 + low : 8 + high, :] = vcode_ref[low:high, :].astype(F32) / 255.0 * vscale_ref[j]

    def pack_group(i):
        loads[2 * i].wait()

        def body(k, carry):
            for u in range(4):
                at = pl.multiple_of(2 * i * GROUP + k * 8192 + u * 2048, 2048)
                pack[i, pl.ds(pl.multiple_of(k * 64 + u * 16, 16), 16), :] = raw[:, pl.ds(at, 2048)].reshape(16, 128)
            return carry

        lax.fori_loop(0, 16, body, 0)

    pack_group(0)
    pl.semaphore_wait(barrier, len(peers))
    edges = [
        send(old.at[:, pl.ds(64, 8), :], old.at[:, pl.ds(0, 8), :], edge_sem, (0,), flat(1)),
        send(old.at[:, pl.ds(8, 8), :], old.at[:, pl.ds(72, 8), :], edge_sem, (1,), flat(-1)),
    ]
    swaps = []
    for i in range(8):
        if i:
            pack_group(i)
        swaps.append(send(pack.at[i], got.at[i], core_sem, (i,), rel(dc=1)))

    rings = (
        (sa, ra, ring_a, NX, x, "dx", RA),
        (sb, rb, ring_b, NY, y, "dy", RB),
        (sc, rc, ring_c, NZ, z, "dz", RC),
    )
    copies = {}

    def ring_step(part, event):
        total, slots, sems, n, here, name, rows = rings[part]
        half = total.shape[1] // 2
        long, k = ring_sends(n)[event]
        for d, step in enumerate((1, -1)):
            which = (0 if long else 1) if d == 0 else (1 if long else 0)
            target = lax.rem(here + step * k + n, n)
            mine = total.at[target, pl.ds(which * half, half), :]
            if (part, d, long, k + 1) in copies:
                copies[part, d, long, k + 1].wait_recv()
                index = [e for e, v in enumerate(ring_sends(n)) if v == (long, k + 1)][0]
                src = slots.at[d, index]
                add_into(src, mine, half, 64)
            else:
                src = mine
            copies[part, d, long, k] = send(src, slots.at[d, event], sems, (d, event), rel(**{name: step}))

    def ring_end(part, long):
        total, slots, sems, n, here, name, rows = rings[part]
        half = total.shape[1] // 2
        index = [e for e, v in enumerate(ring_sends(n)) if v == (long, 1)][0]
        for d in range(2):
            which = (0 if long else 1) if d == 0 else (1 if long else 0)
            copies[part, d, long, 1].wait_recv()
            add_into(total.at[here, pl.ds(which * half, half), :], slots.at[d, index], half, 64)

    for i in range(8):
        group_x = lax.rem(x + X_OFFSETS[i // 2], NX)
        loads[2 * i + 1].wait()
        swaps[i].wait_recv()

        def body(j, carry, i=i, group_x=group_x):
            jy = lax.div(j, 4)
            jz = lax.rem(j, 4) + (i % 2) * 4
            for u in range(4):
                other = got[i, pl.ds(pl.multiple_of(j * 64 + u * 16, 16), 16), :].astype(F32)
                for v in range(2):
                    at = pl.multiple_of((2 * i + 1) * GROUP + j * 8192 + u * 2048 + v * 1024, 1024)
                    row = u * 16 + v * 8
                    both = raw[:, pl.ds(at, 1024)].astype(F32).reshape(8, 128) + other[v * 8 : v * 8 + 8]
                    if row < RA:
                        sa[group_x, pl.ds(pl.multiple_of((jy * NZ + jz) * RA + row, 8), 8), :] = both
                    elif row < RA + RB:
                        sb[jy, pl.ds(pl.multiple_of((group_x * NZ + jz) * RB + row - RA, 8), 8), :] = both
                    else:
                        sc[jz, pl.ds(pl.multiple_of((group_x * NY + jy) * RC + row - RA - RB, 8), 8), :] = both
            return carry

        lax.fori_loop(0, 16, body, 0)
        if i == 1:
            ring_step(0, 0)
        if i == 5:
            ring_step(0, 1)
    ring_step(2, 0)
    ring_step(1, 0)
    ring_step(2, 1)
    ring_step(1, 1)
    ring_step(2, 2)
    ring_step(2, 3)
    ring_step(0, 2)
    ring_step(1, 2)
    ring_step(2, 4)
    ring_step(2, 5)
    ring_step(2, 6)
    ring_end(0, 0)
    ring_end(1, 0)
    ring_end(2, 0)
    ring_end(2, 1)

    def second_send(part, total, here, slots, there, n, name, size):
        out = []
        for d in range(1, n):
            to = lax.rem(there + d, n)
            src = total.at[here, pl.ds(pl.multiple_of(to * size, 8), size), :]
            out.append(send(src, slots.at[d - 1], two_sem, (part, d - 1), rel(**{name: d})))
        return out

    def second_add(waits, total, here, slots, there, n, size):
        for copy in waits:
            copy.wait_recv()

        def body(i, carry):
            at = pl.ds(pl.multiple_of(i * 32, 32), 32)
            own = pl.ds(pl.multiple_of(there * size + i * 32, 8), 32)
            value = total[here, own, :]
            for d in range(n - 1):
                value = value + slots[d, at, :]
            total[here, own, :] = value
            return carry

        lax.fori_loop(0, size // 32, body, 0)

    two_c = second_send(2, sc, z, c2, x, NX, "dx", NY * RC)
    ring_end(0, 1)
    two_a = second_send(0, sa, x, a2, y, NY, "dy", NZ * RA)
    ring_end(1, 1)
    two_b = second_send(1, sb, y, b2, x, NX, "dx", NZ * RB)

    def third_send(total, here, base, slots, sems, there, n, name, size):
        out = []
        for d in range(1, n):
            to = lax.rem(there + d, n)
            src = total.at[here, pl.ds(pl.multiple_of(base + to * size, 8), size), :]
            out.append(send(src, slots.at[d - 1], sems, (d - 1,), rel(**{name: d})))
        return out

    def third_add(waits, total, here, base, slots, there, n, size, row):
        value = total[here, pl.ds(pl.multiple_of(base + there * size, 8), size), :]
        for d, copy in enumerate(waits):
            copy.wait_recv()
            value = value + slots[d]
        gs[8 + row : 8 + row + size, :] = value
        square = value * value
        return sum(square[8 * q : 8 * q + 8] for q in range(size // 8))

    second_add(two_c, sc, z, c2, x, NX, NY * RC)
    three_cs = third_send(sc, z, x * (NY * RC), c3, three_c, y, NY, "dy", RC)
    second_add(two_a, sa, x, a2, y, NY, NZ * RA)
    three_as = third_send(sa, x, y * (NZ * RA), a3, three_a, z, NZ, "dz", RA)
    second_add(two_b, sb, y, b2, x, NX, NZ * RB)
    three_bs = third_send(sb, y, x * (NZ * RB), b3, three_b, z, NZ, "dz", RB)
    square = third_add(three_cs, sc, z, x * (NY * RC), c3, y, NY, RC, RA + RB)
    square = square + third_add(three_as, sa, x, y * (NZ * RA), a3, z, NZ, RA, 0)
    square = square + third_add(three_bs, sb, y, x * (NZ * RB), b3, z, NZ, RB, RA)

    n1[...] = square
    norm1 = [
        send(n1, n1r.at[i], norm1_sem, (i,), rel(dx=dx, dy=dy)) for i, (dx, dy) in enumerate(XY_PEERS)
    ]
    rims = [
        send(gs.at[pl.ds(64, 8), :], gs.at[pl.ds(0, 8), :], edge_sem, (2,), flat(1)),
        send(gs.at[pl.ds(8, 8), :], gs.at[pl.ds(72, 8), :], edge_sem, (3,), flat(-1)),
    ]
    for i, copy in enumerate(norm1):
        copy.wait_recv()
        square = square + n1r[i]
    n2[...] = square
    norm2 = [
        send(n2, n2r.at[i], norm2_sem, (i,), rel(dz=dz, dc=dc)) for i, (dz, dc) in enumerate(ZC_PEERS)
    ]
    count = jnp.full((8, 128), step_ref[0].astype(F32), F32)
    first_fix = 1.0 - jnp.exp(count * math.log(0.9))
    second_fix = 1.0 - jnp.exp(count * math.log(0.95))
    for copy in edges + rims:
        copy.wait_recv()
    for i, copy in enumerate(norm2):
        copy.wait_recv()
        square = square + n2r[i]
    norm = jnp.sqrt(jnp.full((8, 128), jnp.sum(square), F32))
    clip = jnp.minimum(1.0, TOTAL**0.5 / (norm + 1e-06))

    def moments(row):
        scaled = gs[row : row + 8, :] * clip
        momentum = 0.9 * old[0, row : row + 8, :] + 0.1 * scaled
        variance = 0.95 * old[1, row : row + 8, :] + 0.05 * scaled * scaled
        return momentum, variance

    pairs = [moments(8 * q) for q in range(10)]
    for q in range(8):
        momentum, variance = pairs[q + 1]
        update = momentum / first_fix / (jnp.sqrt(variance / second_fix) + 1e-08)
        up_ref[8 * q : 8 * q + 8, :] = update
        new_ref[8 * q : 8 * q + 8, :] = master_ref[8 * q : 8 * q + 8, :] * (1.0 - 0.0001 * 0.1) - 0.0001 * update
    own_rows = pl.ds(pl.multiple_of(r * ROWS, ROWS), ROWS)
    w_ref[own_rows, :] = new_ref[...].astype(BF16)
    gathers = [
        send(w_ref.at[own_rows, :], w_ref.at[own_rows, :], out_sem, (i,), in_rep(dy, dl))
        for i, (dy, dl) in enumerate(REP_PEERS)
    ]
    first = (o > 0).astype(F32)
    last = (o < 255).astype(F32)
    for j in range(5):
        (ma, va), (mb, vb) = pairs[2 * j], pairs[2 * j + 1]
        ma, va, mb, vb = jnp.abs(ma), jnp.abs(va), jnp.abs(mb), jnp.abs(vb)
        if j == 0:
            ma, va = ma * first, va * first
        if j == 4:
            mb, vb = mb * last, vb * last
        m_max = jnp.max(jnp.maximum(ma, mb))
        v_max = jnp.max(jnp.maximum(va, vb))
        am_ref[j] = m_max
        av_ref[j] = v_max
        for q in (2 * j - 1, 2 * j):
            if 0 <= q < 8:
                mn_ref[8 * q : 8 * q + 8, :] = pairs[q + 1][0] / (m_max + 1e-06)
                vn_ref[8 * q : 8 * q + 8, :] = pairs[q + 1][1] / (v_max + 1e-06)
    for copy in gathers:
        copy.wait_recv()
    for copy in started:
        copy.wait_send()


def on_device(grads, momentum_codes, variance_codes, momentum_scale, variance_scale, master, step):
    vmem = pl.BlockSpec(memory_space=pltpu.VMEM)
    smem = pl.BlockSpec(memory_space=pltpu.SMEM)
    tile = jax.ShapeDtypeStruct((ROWS, 128), F32)
    dma = pltpu.SemaphoreType.DMA
    new, weights, update, m_norm, v_norm, m_max, v_max = pl.pallas_call(
        kernel,
        out_shape=(
            tile, jax.ShapeDtypeStruct((16 * ROWS, 128), BF16), tile, tile, tile,
            jax.ShapeDtypeStruct((5,), F32), jax.ShapeDtypeStruct((5,), F32),
        ),
        in_specs=[pl.BlockSpec(memory_space=pl.ANY), vmem, vmem, vmem, smem, smem, smem],
        out_specs=(vmem, vmem, vmem, vmem, vmem, smem, smem),
        scratch_shapes=[
            pltpu.VMEM((1, 16 * GROUP), BF16),
            pltpu.VMEM((8, GROUP_ROWS, 128), BF16),
            pltpu.VMEM((8, GROUP_ROWS, 128), BF16),
            pltpu.VMEM((NX, NY * NZ * RA, 128), F32),
            pltpu.VMEM((NY, NX * NZ * RB, 128), F32),
            pltpu.VMEM((NZ, NX * NY * RC, 128), F32),
            pltpu.VMEM((2, 3, NY * NZ * RA // 2, 128), F32),
            pltpu.VMEM((2, 3, NX * NZ * RB // 2, 128), F32),
            pltpu.VMEM((2, 7, NX * NY * RC // 2, 128), F32),
            pltpu.VMEM((NY - 1, NZ * RA, 128), F32),
            pltpu.VMEM((NX - 1, NZ * RB, 128), F32),
            pltpu.VMEM((NX - 1, NY * RC, 128), F32),
            pltpu.VMEM((NZ - 1, RA, 128), F32),
            pltpu.VMEM((NZ - 1, RB, 128), F32),
            pltpu.VMEM((NY - 1, RC, 128), F32),
            pltpu.VMEM((80, 128), F32),
            pltpu.VMEM((2, 80, 128), F32),
            pltpu.VMEM((8, 128), F32),
            pltpu.VMEM((8, 128), F32),
            pltpu.VMEM((15, 8, 128), F32),
            pltpu.VMEM((15, 8, 128), F32),
            dma((16,)), dma((2, 8)), dma((2, 2, 3)), dma((2, 2, 3)), dma((2, 2, 7)), dma((2, 3, 3)),
            dma((2, 7)), dma((2, 7)), dma((2, 3)),
            dma((2, 4)), dma((2, 15)), dma((2, 15)), dma((2, 15)),
        ],
        compiler_params=pltpu.CompilerParams(
            collective_id=0, has_side_effects=True, vmem_limit_bytes=48 * 2**20
        ),
        name="adam_window",
    )(
        grads, momentum_codes.reshape(ROWS, 128), variance_codes.reshape(ROWS, 128), master.reshape(ROWS, 128),
        momentum_scale, variance_scale, step,
    )
    return (
        new.reshape(-1), weights.reshape(-1), update.reshape(-1), m_norm.reshape(-1), v_norm.reshape(-1), m_max, v_max
    )


def solution(mesh):
    own = P(("shard", "rep"))
    return jax.shard_map(
        on_device,
        mesh=mesh,
        in_specs=(P("shard", "rep", None), own, own, own, own, own, P()),
        out_specs=(own, P("shard"), own, own, own, own, own),
        check_vma=False,
    )
```

```python
import functools
import math

import jax
import jax.numpy as jnp
from jax import lax
from jax.experimental import pallas as pl
from jax.experimental.pallas import tpu as pltpu
from jax.sharding import PartitionSpec as P

MESH = pl.DeviceIdType.MESH
F32 = jnp.float32
BF16 = jnp.bfloat16

NX, NY, NZ = 4, 4, 8
ROWS = 64
PART_ROWS = (24, 24, 16)
RA, RB, RC = PART_ROWS
TOTAL = float(NX * NY * NZ * 2 * ROWS * 128)
GROUP = 131072
GROUP_ROWS = GROUP // 128

X_OFFSETS = (2, 1, 3, 0)
XY_PEERS = [(dx, dy) for dx in range(NX) for dy in range(NY) if dx or dy]
ZC_PEERS = [(dz, dc) for dz in range(NZ) for dc in range(2) if dz or dc]
REP_PEERS = [(dy, dl) for dy in range(4) for dl in range(4) if dy or dl]


def ring_sends(n):
    order = []
    for step in range(n // 2):
        order.append((1, n // 2 - step))
        if n // 2 - 1 - step >= 1:
            order.append((0, n // 2 - 1 - step))
    return order


def device(x, y, z, c):
    return ((x * 2 + lax.div(z, 4)) * 2 + c, y * 4 + lax.rem(z, 4))


def add_into(dst, src, rows, tile):
    def body(i, carry):
        at = pl.ds(pl.multiple_of(i * tile, tile), tile)
        dst[at, :] = dst[at, :] + src[at, :]
        return carry

    lax.fori_loop(0, rows // tile, body, 0)


def kernel(
    g_ref, mcode_ref, vcode_ref, master_ref, mscale_ref, vscale_ref, step_ref,
    new_ref, w_ref, up_ref, mn_ref, vn_ref, am_ref, av_ref,
    raw, pack, got, sa, sb, sc, ra, rb, rc, a2, b2, c2, a3, b3, c3,
    gs, old, n1, n2, n1r, n2r,
    load_sem, core_sem, ring_a, ring_b, ring_c, two_sem, three_a, three_b, three_c,
    edge_sem, norm1_sem, norm2_sem, out_sem,
):
    s, r = lax.axis_index("shard"), lax.axis_index("rep")
    x, c = lax.div(s, 4), lax.rem(s, 2)
    y, zl = lax.div(r, 4), lax.rem(r, 4)
    zh = lax.rem(lax.div(s, 2), 2)
    z = zh * 4 + zl
    o = s * 16 + r

    def rel(dx=0, dy=0, dz=0, dc=0):
        return device(
            lax.rem(x + dx + NX, NX), lax.rem(y + dy + NY, NY), lax.rem(z + dz + NZ, NZ), lax.rem(c + dc, 2)
        )

    def in_rep(dy, dl):
        return (s, lax.rem(y + dy, 4) * 4 + lax.rem(zl + dl, 4))

    def flat(step):
        to = lax.rem(o + step + 256, 256)
        return (lax.div(to, 16), lax.rem(to, 16))

    def remote(src, dst, sems, index, to):
        return pltpu.make_async_remote_copy(
            src_ref=src, dst_ref=dst, send_sem=sems.at[(0,) + index], recv_sem=sems.at[(1,) + index],
            device_id=to, device_id_type=MESH,
        )

    started = []

    def send(src, dst, sems, index, to):
        copy = remote(src, dst, sems, index, to)
        copy.start()
        started.append(copy)
        return copy

    loads = []
    for i in range(8):
        group = lax.rem(x + X_OFFSETS[i // 2], NX) * 2 + i % 2
        for own in (0, 1):
            core = c if own else 1 - c
            at = pl.multiple_of((group * 2 + core) * GROUP, GROUP)
            load = pltpu.make_async_copy(
                g_ref.at[0, :, pl.ds(at, GROUP)], raw.at[:, pl.ds((2 * i + own) * GROUP, GROUP)], load_sem.at[2 * i + own]
            )
            load.start()
            loads.append(load)

    barrier = pltpu.get_barrier_semaphore()
    peers = [rel(dc=1), rel(dx=1), rel(dx=-1), rel(dy=1), rel(dy=-1), rel(dz=1), rel(dz=-1)]
    for peer in peers:
        pl.semaphore_signal(barrier, inc=1, device_id=peer, device_id_type=MESH)

    for j in range(5):
        low, high = max(16 * j - 8, 0), min(16 * j + 8, ROWS)
        old[0, 8 + low : 8 + high, :] = mcode_ref[low:high, :].astype(F32) / 127.0 * mscale_ref[j]
        old[1, 8 + low : 8 + high, :] = vcode_ref[low:high, :].astype(F32) / 255.0 * vscale_ref[j]

    def pack_group(i):
        loads[2 * i].wait()

        def body(k, carry):
            for u in range(4):
                at = pl.multiple_of(2 * i * GROUP + k * 8192 + u * 2048, 2048)
                pack[i, pl.ds(pl.multiple_of(k * 64 + u * 16, 16), 16), :] = raw[:, pl.ds(at, 2048)].reshape(16, 128)
            return carry

        lax.fori_loop(0, 16, body, 0)

    pack_group(0)
    pl.semaphore_wait(barrier, len(peers))
    swaps = []
    for i in range(8):
        if i:
            pack_group(i)
        swaps.append(send(pack.at[i], got.at[i], core_sem, (i,), rel(dc=1)))

    rings = (
        (sa, ra, ring_a, NX, x, "dx", RA),
        (sb, rb, ring_b, NY, y, "dy", RB),
        (sc, rc, ring_c, NZ, z, "dz", RC),
    )
    copies = {}

    def ring_step(part, event):
        total, slots, sems, n, here, name, rows = rings[part]
        half = total.shape[1] // 2
        long, k = ring_sends(n)[event]
        for d, step in enumerate((1, -1)):
            which = (0 if long else 1) if d == 0 else (1 if long else 0)
            target = lax.rem(here + step * k + n, n)
            mine = total.at[target, pl.ds(which * half, half), :]
            if (part, d, long, k + 1) in copies:
                copies[part, d, long, k + 1].wait_recv()
                index = [e for e, v in enumerate(ring_sends(n)) if v == (long, k + 1)][0]
                src = slots.at[d, index]
                add_into(src, mine, half, 64)
            else:
                src = mine
            copies[part, d, long, k] = send(src, slots.at[d, event], sems, (d, event), rel(**{name: step}))

    def ring_end(part, long):
        total, slots, sems, n, here, name, rows = rings[part]
        half = total.shape[1] // 2
        index = [e for e, v in enumerate(ring_sends(n)) if v == (long, 1)][0]
        for d in range(2):
            which = (0 if long else 1) if d == 0 else (1 if long else 0)
            copies[part, d, long, 1].wait_recv()
            add_into(total.at[here, pl.ds(which * half, half), :], slots.at[d, index], half, 64)

    for i in range(8):
        group_x = lax.rem(x + X_OFFSETS[i // 2], NX)
        loads[2 * i + 1].wait()
        swaps[i].wait_recv()

        def body(j, carry, i=i, group_x=group_x):
            jy = lax.div(j, 4)
            jz = lax.rem(j, 4) + (i % 2) * 4
            for u in range(4):
                other = got[i, pl.ds(pl.multiple_of(j * 64 + u * 16, 16), 16), :].astype(F32)
                for v in range(2):
                    at = pl.multiple_of((2 * i + 1) * GROUP + j * 8192 + u * 2048 + v * 1024, 1024)
                    row = u * 16 + v * 8
                    both = raw[:, pl.ds(at, 1024)].astype(F32).reshape(8, 128) + other[v * 8 : v * 8 + 8]
                    if row < RA:
                        sa[group_x, pl.ds(pl.multiple_of((jy * NZ + jz) * RA + row, 8), 8), :] = both
                    elif row < RA + RB:
                        sb[jy, pl.ds(pl.multiple_of((group_x * NZ + jz) * RB + row - RA, 8), 8), :] = both
                    else:
                        sc[jz, pl.ds(pl.multiple_of((group_x * NY + jy) * RC + row - RA - RB, 8), 8), :] = both
            return carry

        lax.fori_loop(0, 16, body, 0)
        if i == 1:
            ring_step(0, 0)
        if i == 5:
            ring_step(0, 1)
    ring_step(2, 0)
    ring_step(1, 0)
    ring_step(2, 1)
    ring_step(1, 1)
    ring_step(2, 2)
    ring_step(2, 3)
    ring_step(0, 2)
    ring_step(1, 2)
    ring_step(2, 4)
    ring_step(2, 5)
    ring_step(2, 6)
    ring_end(0, 0)
    ring_end(1, 0)
    ring_end(2, 0)
    ring_end(2, 1)

    def second_send(part, total, here, slots, there, n, name, size):
        out = []
        for d in range(1, n):
            to = lax.rem(there + d, n)
            src = total.at[here, pl.ds(pl.multiple_of(to * size, 8), size), :]
            out.append(send(src, slots.at[d - 1], two_sem, (part, d - 1), rel(**{name: d})))
        return out

    def second_add(waits, total, here, slots, there, n, size):
        for copy in waits:
            copy.wait_recv()

        def body(i, carry):
            at = pl.ds(pl.multiple_of(i * 32, 32), 32)
            own = pl.ds(pl.multiple_of(there * size + i * 32, 8), 32)
            value = total[here, own, :]
            for d in range(n - 1):
                value = value + slots[d, at, :]
            total[here, own, :] = value
            return carry

        lax.fori_loop(0, size // 32, body, 0)

    two_c = second_send(2, sc, z, c2, x, NX, "dx", NY * RC)
    ring_end(0, 1)
    two_a = second_send(0, sa, x, a2, y, NY, "dy", NZ * RA)
    ring_end(1, 1)
    two_b = second_send(1, sb, y, b2, x, NX, "dx", NZ * RB)

    def third_send(total, here, base, slots, sems, there, n, name, size):
        out = []
        for d in range(1, n):
            to = lax.rem(there + d, n)
            src = total.at[here, pl.ds(pl.multiple_of(base + to * size, 8), size), :]
            out.append(send(src, slots.at[d - 1], sems, (d - 1,), rel(**{name: d})))
        return out

    def third_add(waits, total, here, base, slots, there, n, size, row):
        value = total[here, pl.ds(pl.multiple_of(base + there * size, 8), size), :]
        for d, copy in enumerate(waits):
            copy.wait_recv()
            value = value + slots[d]
        gs[8 + row : 8 + row + size, :] = value
        square = value * value
        return sum(square[8 * q : 8 * q + 8] for q in range(size // 8))

    second_add(two_c, sc, z, c2, x, NX, NY * RC)
    three_cs = third_send(sc, z, x * (NY * RC), c3, three_c, y, NY, "dy", RC)
    second_add(two_a, sa, x, a2, y, NY, NZ * RA)
    three_as = third_send(sa, x, y * (NZ * RA), a3, three_a, z, NZ, "dz", RA)
    second_add(two_b, sb, y, b2, x, NX, NZ * RB)
    three_bs = third_send(sb, y, x * (NZ * RB), b3, three_b, z, NZ, "dz", RB)
    square = third_add(three_cs, sc, z, x * (NY * RC), c3, y, NY, RC, RA + RB)
    square = square + third_add(three_as, sa, x, y * (NZ * RA), a3, z, NZ, RA, 0)
    square = square + third_add(three_bs, sb, y, x * (NZ * RB), b3, z, NZ, RB, RA)

    n1[...] = square
    norm1 = [
        send(n1, n1r.at[i], norm1_sem, (i,), rel(dx=dx, dy=dy)) for i, (dx, dy) in enumerate(XY_PEERS)
    ]
    edges = [
        send(old.at[:, pl.ds(64, 8), :], old.at[:, pl.ds(0, 8), :], edge_sem, (0,), flat(1)),
        send(old.at[:, pl.ds(8, 8), :], old.at[:, pl.ds(72, 8), :], edge_sem, (1,), flat(-1)),
    ]
    rims = [
        send(gs.at[pl.ds(64, 8), :], gs.at[pl.ds(0, 8), :], edge_sem, (2,), flat(1)),
        send(gs.at[pl.ds(8, 8), :], gs.at[pl.ds(72, 8), :], edge_sem, (3,), flat(-1)),
    ]
    for i, copy in enumerate(norm1):
        copy.wait_recv()
        square = square + n1r[i]
    n2[...] = square
    norm2 = [
        send(n2, n2r.at[i], norm2_sem, (i,), rel(dz=dz, dc=dc)) for i, (dz, dc) in enumerate(ZC_PEERS)
    ]
    count = jnp.full((8, 128), step_ref[0].astype(F32), F32)
    first_fix = 1.0 - jnp.exp(count * math.log(0.9))
    second_fix = 1.0 - jnp.exp(count * math.log(0.95))
    for copy in edges + rims:
        copy.wait_recv()
    for i, copy in enumerate(norm2):
        copy.wait_recv()
        square = square + n2r[i]
    norm = jnp.sqrt(jnp.full((8, 128), jnp.sum(square), F32))
    clip = jnp.minimum(1.0, TOTAL**0.5 / (norm + 1e-06))

    def moments(row):
        scaled = gs[row : row + 8, :] * clip
        momentum = 0.9 * old[0, row : row + 8, :] + 0.1 * scaled
        variance = 0.95 * old[1, row : row + 8, :] + 0.05 * scaled * scaled
        return momentum, variance

    pairs = [moments(8 * q) for q in range(10)]
    for q in range(8):
        momentum, variance = pairs[q + 1]
        update = momentum / first_fix / (jnp.sqrt(variance / second_fix) + 1e-08)
        up_ref[8 * q : 8 * q + 8, :] = update
        new_ref[8 * q : 8 * q + 8, :] = master_ref[8 * q : 8 * q + 8, :] * (1.0 - 0.0001 * 0.1) - 0.0001 * update
    own_rows = pl.ds(pl.multiple_of(r * ROWS, ROWS), ROWS)
    w_ref[own_rows, :] = new_ref[...].astype(BF16)
    gathers = [
        send(w_ref.at[own_rows, :], w_ref.at[own_rows, :], out_sem, (i,), in_rep(dy, dl))
        for i, (dy, dl) in enumerate(REP_PEERS)
    ]
    first = (o > 0).astype(F32)
    last = (o < 255).astype(F32)
    for j in range(5):
        (ma, va), (mb, vb) = pairs[2 * j], pairs[2 * j + 1]
        ma, va, mb, vb = jnp.abs(ma), jnp.abs(va), jnp.abs(mb), jnp.abs(vb)
        if j == 0:
            ma, va = ma * first, va * first
        if j == 4:
            mb, vb = mb * last, vb * last
        m_max = jnp.max(jnp.maximum(ma, mb))
        v_max = jnp.max(jnp.maximum(va, vb))
        am_ref[j] = m_max
        av_ref[j] = v_max
        for q in (2 * j - 1, 2 * j):
            if 0 <= q < 8:
                mn_ref[8 * q : 8 * q + 8, :] = pairs[q + 1][0] / (m_max + 1e-06)
                vn_ref[8 * q : 8 * q + 8, :] = pairs[q + 1][1] / (v_max + 1e-06)
    for copy in gathers:
        copy.wait_recv()
    for copy in started:
        copy.wait_send()


def on_device(grads, momentum_codes, variance_codes, momentum_scale, variance_scale, master, step):
    vmem = pl.BlockSpec(memory_space=pltpu.VMEM)
    smem = pl.BlockSpec(memory_space=pltpu.SMEM)
    tile = jax.ShapeDtypeStruct((ROWS, 128), F32)
    dma = pltpu.SemaphoreType.DMA
    new, weights, update, m_norm, v_norm, m_max, v_max = pl.pallas_call(
        kernel,
        out_shape=(
            tile, jax.ShapeDtypeStruct((16 * ROWS, 128), BF16), tile, tile, tile,
            jax.ShapeDtypeStruct((5,), F32), jax.ShapeDtypeStruct((5,), F32),
        ),
        in_specs=[pl.BlockSpec(memory_space=pl.ANY), vmem, vmem, vmem, smem, smem, smem],
        out_specs=(vmem, vmem, vmem, vmem, vmem, smem, smem),
        scratch_shapes=[
            pltpu.VMEM((1, 16 * GROUP), BF16),
            pltpu.VMEM((8, GROUP_ROWS, 128), BF16),
            pltpu.VMEM((8, GROUP_ROWS, 128), BF16),
            pltpu.VMEM((NX, NY * NZ * RA, 128), F32),
            pltpu.VMEM((NY, NX * NZ * RB, 128), F32),
            pltpu.VMEM((NZ, NX * NY * RC, 128), F32),
            pltpu.VMEM((2, 3, NY * NZ * RA // 2, 128), F32),
            pltpu.VMEM((2, 3, NX * NZ * RB // 2, 128), F32),
            pltpu.VMEM((2, 7, NX * NY * RC // 2, 128), F32),
            pltpu.VMEM((NY - 1, NZ * RA, 128), F32),
            pltpu.VMEM((NX - 1, NZ * RB, 128), F32),
            pltpu.VMEM((NX - 1, NY * RC, 128), F32),
            pltpu.VMEM((NZ - 1, RA, 128), F32),
            pltpu.VMEM((NZ - 1, RB, 128), F32),
            pltpu.VMEM((NY - 1, RC, 128), F32),
            pltpu.VMEM((80, 128), F32),
            pltpu.VMEM((2, 80, 128), F32),
            pltpu.VMEM((8, 128), F32),
            pltpu.VMEM((8, 128), F32),
            pltpu.VMEM((15, 8, 128), F32),
            pltpu.VMEM((15, 8, 128), F32),
            dma((16,)), dma((2, 8)), dma((2, 2, 3)), dma((2, 2, 3)), dma((2, 2, 7)), dma((2, 3, 3)),
            dma((2, 7)), dma((2, 7)), dma((2, 3)),
            dma((2, 4)), dma((2, 15)), dma((2, 15)), dma((2, 15)),
        ],
        compiler_params=pltpu.CompilerParams(
            collective_id=0, has_side_effects=True, vmem_limit_bytes=48 * 2**20
        ),
        name="adam_window",
    )(
        grads, momentum_codes.reshape(ROWS, 128), variance_codes.reshape(ROWS, 128), master.reshape(ROWS, 128),
        momentum_scale, variance_scale, step,
    )
    return (
        new.reshape(-1), weights.reshape(-1), update.reshape(-1), m_norm.reshape(-1), v_norm.reshape(-1), m_max, v_max
    )


def solution(mesh):
    own = P(("shard", "rep"))
    return jax.shard_map(
        on_device,
        mesh=mesh,
        in_specs=(P("shard", "rep", None), own, own, own, own, own, P()),
        out_specs=(own, P("shard"), own, own, own, own, own),
        check_vma=False,
    )
```

```python
import math

import jax
import jax.numpy as jnp
from jax import lax
from jax.experimental import pallas as pl
from jax.experimental.pallas import tpu as pltpu
from jax.sharding import PartitionSpec as P

MESH = pl.DeviceIdType.MESH
F32 = jnp.float32
BF16 = jnp.bfloat16

NX, NY, NZ = 4, 4, 8
SIZES = {"x": NX, "y": NY, "z": NZ, "c": 2}
ROWS = 64
TOTAL = float(NX * NY * NZ * 2 * ROWS * 128)
GROUP = 131072
GROUP_ROWS = GROUP // 128

PARTS = (("xyz", 0, 16), ("yxz", 16, 16), ("zxy", 32, 16), ("xyz", 48, 8), ("yxz", 56, 8))

X_OFFSETS = (2, 1, 3, 0)
PLACE = {d: i for i, d in enumerate(X_OFFSETS)}


XY_PEERS = ((2, 2), (1, 2), (2, 1), (2, 3), (3, 2), (0, 2), (1, 1), (1, 3), (2, 0), (3, 1), (3, 3), (0, 1), (0, 3), (1, 0), (3, 0))
ZC_PEERS = ((4, 1), (4, 0), (3, 1), (5, 1), (3, 0), (5, 0), (2, 1), (6, 1), (2, 0), (6, 0), (1, 1), (7, 1), (1, 0), (7, 0), (0, 1))
REP_PEERS = ((2, 3), (1, 3), (2, 2), (3, 3), (0, 3), (1, 2), (2, 1), (3, 2), (0, 2), (1, 1), (2, 0), (3, 1), (0, 1), (1, 0), (3, 0))
FAR_FIRST = {4: (2, 1, 3), 8: (4, 3, 5, 2, 6, 1, 7)}


def ring_sends(n):
    order = []
    for step in range(n // 2):
        order.append((1, n // 2 - step))
        if n // 2 - 1 - step >= 1:
            order.append((0, n // 2 - 1 - step))
    return order


def half_of(d, long):
    return 1 - long if d == 0 else long


PACK, SUM, RING, END, SECOND, THIRD, LAST = range(7)
ORDER = (
    (PACK, 0), (PACK, 1), (PACK, 2), (PACK, 3), (PACK, 4), (SUM, 0), (PACK, 5), (PACK, 6), (PACK, 7), (SUM, 1),
    (RING, 0, 0, 1, 2), (RING, 0, 1, 1, 2), (RING, 3, 0, 1, 2), (RING, 3, 1, 1, 2), (SUM, 2), (SUM, 3),
    (RING, 0, 0, 0, 1), (RING, 1, 0, 1, 2), (RING, 1, 1, 0, 1), (RING, 2, 0, 1, 4), (RING, 2, 1, 0, 3),
    (RING, 3, 0, 0, 1), (RING, 4, 0, 1, 2), (RING, 4, 1, 0, 1), (SUM, 4), (SUM, 5), (RING, 0, 1, 0, 1),
    (RING, 3, 1, 0, 1), (SUM, 6), (SUM, 7), (RING, 1, 0, 0, 1), (RING, 1, 1, 1, 2), (RING, 2, 0, 0, 3),
    (RING, 2, 1, 1, 4), (RING, 4, 0, 0, 1), (RING, 4, 1, 1, 2), (RING, 0, 0, 1, 1), (RING, 0, 1, 1, 1),
    (RING, 2, 0, 1, 3), (RING, 2, 1, 0, 2), (RING, 3, 0, 1, 1), (RING, 1, 0, 1, 1), (RING, 3, 1, 1, 1),
    (END, 1, 1, 0), (RING, 4, 0, 1, 1), (END, 4, 1, 0), (RING, 2, 0, 0, 2), (RING, 2, 1, 1, 3), (END, 0, 0, 0),
    (END, 0, 1, 0), (RING, 2, 0, 1, 2), (RING, 2, 1, 0, 1), (END, 3, 0, 0), (END, 1, 0, 0), (END, 3, 1, 0),
    (RING, 1, 1, 1, 1), (RING, 2, 0, 0, 1), (RING, 2, 1, 1, 2), (END, 4, 0, 0), (RING, 4, 1, 1, 1),
    (RING, 2, 0, 1, 1), (END, 2, 1, 0), (END, 0, 0, 1), (END, 0, 1, 1), (SECOND, 0), (END, 3, 0, 1), (END, 1, 0, 1),
    (END, 3, 1, 1), (SECOND, 3), (END, 2, 0, 0), (RING, 2, 1, 1, 1), (END, 1, 1, 1), (SECOND, 1), (END, 4, 0, 1),
    (END, 2, 0, 1), (END, 4, 1, 1), (SECOND, 4), (END, 2, 1, 1), (SECOND, 2), (THIRD, 0), (THIRD, 1), (THIRD, 3),
    (THIRD, 4), (THIRD, 2), (LAST, 0), (LAST, 2), (LAST, 1), (LAST, 3), (LAST, 4),
)


def device(x, y, z, c):
    return ((x * 2 + lax.div(z, 4)) * 2 + c, y * 4 + lax.rem(z, 4))


def add_into(dst, src, rows, tile=64):
    def body(i, carry):
        at = pl.ds(pl.multiple_of(i * tile, tile), tile)
        dst[at, :] = dst[at, :] + src[at, :]
        return carry

    lax.fori_loop(0, rows // tile, body, 0)


def layout():
    dma = pltpu.SemaphoreType.DMA
    out = {
        "raw": pltpu.VMEM((1, 16 * GROUP), BF16),
        "pack": pltpu.VMEM((8, GROUP_ROWS, 128), BF16),
        "got": pltpu.VMEM((8, GROUP_ROWS, 128), BF16),
        "mcode": pltpu.VMEM((ROWS, 128), jnp.int32),
        "vcode": pltpu.VMEM((ROWS, 128), jnp.int32),
        "master": pltpu.VMEM((ROWS, 128), F32),
        "mscale": pltpu.SMEM((5,), F32),
        "vscale": pltpu.SMEM((5,), F32),
        "step": pltpu.SMEM((1,), jnp.int32),
        "state": pltpu.VMEM((3, 80, 128), F32),
        "out": pltpu.VMEM((4, ROWS, 128), F32),
        "half": pltpu.VMEM((ROWS, 128), BF16),
        "am": pltpu.SMEM((5,), F32),
        "av": pltpu.SMEM((5,), F32),
        "n1": pltpu.VMEM((8, 128), F32),
        "n2": pltpu.VMEM((8, 128), F32),
        "n1r": pltpu.VMEM((15, 8, 128), F32),
        "n2r": pltpu.VMEM((15, 8, 128), F32),
        "load_sem": dma((16,)),
        "input_sem": dma((6,)),
        "core_sem": dma((2, 8)),
        "edge_sem": dma((2, 2)),
        "norm1_sem": dma((2, 15)),
        "norm2_sem": dma((2, 15)),
        "out_sem": dma((2, 15)),
        "leave_sem": dma((7,)),
    }
    for p, (axes, _, rows) in enumerate(PARTS):
        n1, n2, n3 = (SIZES[a] for a in axes)
        out["sum", p] = pltpu.VMEM((n1, n2 * n3 * rows, 128), F32)
        out["ring", p] = pltpu.VMEM((2, n1 - 1, n2 * n3 * rows // 2, 128), F32)
        out["two", p] = pltpu.VMEM((n2 - 1, n3 * rows, 128), F32)
        out["three", p] = pltpu.VMEM((n3 - 1, rows, 128), F32)
        out["ring_sem", p] = dma((2, 2, n1 - 1))
        out["two_sem", p] = dma((2, n2 - 1))
        out["three_sem", p] = dma((2, n3 - 1))
    return out


def kernel(g_ref, mcode_ref, vcode_ref, mscale_ref, vscale_ref, master_ref, step_ref, new_hbm, w_ref, up_hbm, mn_hbm, vn_hbm, am_hbm, av_hbm, *scratches):
    refs = {}
    for name, ref in zip(layout(), scratches):
        refs[name] = ref
    raw, pack, got, state = refs["raw"], refs["pack"], refs["got"], refs["state"]
    s, r = lax.axis_index("shard"), lax.axis_index("rep")
    x, c = lax.div(s, 4), lax.rem(s, 2)
    y, zl = lax.div(r, 4), lax.rem(r, 4)
    z = lax.rem(lax.div(s, 2), 2) * 4 + zl
    here = {"x": x, "y": y, "z": z}
    o = s * 16 + r

    def rel(*moves):
        at = {"x": x, "y": y, "z": z, "c": c}
        for axis, by in moves:
            at[axis] = lax.rem(at[axis] + by + SIZES[axis], SIZES[axis])
        return device(at["x"], at["y"], at["z"], at["c"])

    def in_rep(dy, dl):
        return (s, lax.rem(y + dy, 4) * 4 + lax.rem(zl + dl, 4))

    def flat(step):
        to = lax.rem(o + step + 256, 256)
        return (lax.div(to, 16), lax.rem(to, 16))

    started = []

    def send(src, dst, sems, index, to):
        copy = pltpu.make_async_remote_copy(
            src_ref=src, dst_ref=dst, send_sem=sems.at[(0,) + index], recv_sem=sems.at[(1,) + index],
            device_id=to, device_id_type=MESH,
        )
        copy.start()
        started.append(copy)
        return copy

    barrier = pltpu.get_barrier_semaphore()
    peers = [rel(("c", 1))] + [rel((a, d)) for a in "xyz" for d in (1, -1)]
    for peer in peers:
        pl.semaphore_signal(barrier, inc=1, device_id=peer, device_id_type=MESH)

    loads = []
    for i in range(8):
        group = lax.rem(x + X_OFFSETS[i // 2], NX) * 2 + i % 2
        for own in (0, 1):
            core = c if own else 1 - c
            at = pl.multiple_of((group * 2 + core) * GROUP, GROUP)
            load = pltpu.make_async_copy(
                g_ref.at[0, :, pl.ds(at, GROUP)],
                raw.at[:, pl.ds((2 * i + own) * GROUP, GROUP)],
                refs["load_sem"].at[2 * i + own],
            )
            load.start()
            loads.append(load)
    inputs = []
    for i, (src, name) in enumerate(
        (
            (mcode_ref, "mcode"), (vcode_ref, "vcode"), (master_ref, "master"),
            (mscale_ref, "mscale"), (vscale_ref, "vscale"), (step_ref, "step"),
        )
    ):
        copy = pltpu.make_async_copy(src, refs[name], refs["input_sem"].at[i])
        copy.start()
        inputs.append(copy)

    swaps = {}

    def pack_step(i):
        loads[2 * i].wait()

        def body(k, carry):
            for u in range(4):
                at = pl.multiple_of(2 * i * GROUP + k * 8192 + u * 2048, 2048)
                pack[i, pl.ds(pl.multiple_of(k * 64 + u * 16, 16), 16), :] = raw[:, pl.ds(at, 2048)].reshape(16, 128)
            return carry

        lax.fori_loop(0, 16, body, 0)
        if i == 0:
            pl.semaphore_wait(barrier, len(peers))
        swaps[i] = send(pack.at[i], got.at[i], refs["core_sem"], (i,), rel(("c", 1)))

    def group_step(i):
        loads[2 * i + 1].wait()
        swaps[i].wait_recv()
        place = i // 2

        def body(j, carry):
            jy = lax.div(j, 4)
            jz = lax.rem(j, 4) + (i % 2) * 4
            for u in range(4):
                other = got[i, pl.ds(pl.multiple_of(j * 64 + u * 16, 16), 16), :].astype(F32)
                for v in range(2):
                    at = pl.multiple_of((2 * i + 1) * GROUP + j * 8192 + u * 2048 + v * 1024, 1024)
                    row = u * 16 + v * 8
                    both = raw[:, pl.ds(at, 1024)].astype(F32).reshape(8, 128) + other[v * 8 : v * 8 + 8]
                    for p, (axes, low, rows) in enumerate(PARTS):
                        if low <= row < low + rows:
                            first, chunk = {
                                "x": (place, jy * NZ + jz),
                                "y": (jy, place * NZ + jz),
                                "z": (jz, place * NY + jy),
                            }[axes[0]]
                            at = pl.ds(pl.multiple_of(chunk * rows + row - low, 8), 8)
                            refs["sum", p][first, at, :] = both
            return carry

        lax.fori_loop(0, 16, body, 0)

    copies = {}

    def first_index(p, distance):
        a = PARTS[p][0][0]
        n = SIZES[a]
        return PLACE[distance % n] if a == "x" else lax.rem(here[a] + distance + n, n)

    def ring_step(p, d, long, k):
        axes = PARTS[p][0]
        total, slots = refs["sum", p], refs["ring", p]
        order = ring_sends(SIZES[axes[0]])
        step = 1 - 2 * d
        half = total.shape[1] // 2
        src = total.at[first_index(p, step * k), pl.ds(half_of(d, long) * half, half), :]
        if (long, k + 1) in order:
            copies[p, d, long, k + 1].wait_recv()
            landed = slots.at[d, order.index((long, k + 1))]
            add_into(landed, src, half)
            src = landed
        event = order.index((long, k))
        copies[p, d, long, k] = send(
            src, slots.at[d, event], refs["ring_sem", p], (d, event), rel((axes[0], step))
        )

    def end_step(p, d, long):
        total, slots = refs["sum", p], refs["ring", p]
        half = total.shape[1] // 2
        copies[p, d, long, 1].wait_recv()
        event = ring_sends(SIZES[PARTS[p][0][0]]).index((long, 1))
        add_into(total.at[first_index(p, 0), pl.ds(half_of(d, long) * half, half), :], slots.at[d, event], half)

    def second_index(p, distance):
        a = PARTS[p][0][1]
        return PLACE[distance % 4] if a == "x" else lax.rem(here[a] + distance, SIZES[a])

    def second_step(p):
        axes, _, rows = PARTS[p]
        size = SIZES[axes[2]] * rows
        for d in FAR_FIRST[SIZES[axes[1]]]:
            src = refs["sum", p].at[first_index(p, 0), pl.ds(pl.multiple_of(second_index(p, d) * size, 8), size), :]
            copies["two", p, d] = send(
                src, refs["two", p].at[d - 1], refs["two_sem", p], (d - 1,), rel((axes[1], d))
            )

    def third_rows(p, distance):
        axes, _, rows = PARTS[p]
        n = SIZES[axes[2]]
        base = second_index(p, 0) * (n * rows)
        return pl.ds(pl.multiple_of(base + lax.rem(here[axes[2]] + distance, n) * rows, 8), rows)

    def third_step(p):
        axes, _, rows = PARTS[p]
        size = SIZES[axes[2]] * rows
        n = SIZES[axes[1]]
        total, slots = refs["sum", p], refs["two", p]
        for d in range(1, n):
            copies["two", p, d].wait_recv()
        first = first_index(p, 0)
        for i in range(size // 32):
            at = pl.ds(pl.multiple_of(second_index(p, 0) * size + i * 32, 8), 32)
            value = total[first, at, :]
            for d in range(1, n):
                value = value + slots[d - 1, i * 32 : i * 32 + 32, :]
            total[first, at, :] = value
        for d in FAR_FIRST[SIZES[axes[2]]]:
            copies["three", p, d] = send(
                total.at[first, third_rows(p, d), :], refs["three", p].at[d - 1], refs["three_sem", p],
                (d - 1,), rel((axes[2], d)),
            )

    squares = []

    def last_step(p):
        axes, low, rows = PARTS[p]
        value = refs["sum", p][first_index(p, 0), third_rows(p, 0), :]
        for d in range(1, SIZES[axes[2]]):
            copies["three", p, d].wait_recv()
        for d in range(1, SIZES[axes[2]]):
            value = value + refs["three", p][d - 1]
        state[2, 8 + low : 8 + low + rows, :] = value
        square = value * value
        squares.extend(square[8 * q : 8 * q + 8] for q in range(rows // 8))

    def old_step():
        for copy in inputs:
            copy.wait()
        for j in range(5):
            low, high = max(16 * j - 8, 0), min(16 * j + 8, ROWS)
            state[0, 8 + low : 8 + high, :] = refs["mcode"][low:high, :].astype(F32) / 127.0 * refs["mscale"][j]
            state[1, 8 + low : 8 + high, :] = refs["vcode"][low:high, :].astype(F32) / 255.0 * refs["vscale"][j]

    did_old = False
    for task in ORDER:
        if task[0] == SECOND and not did_old:
            old_step()
            did_old = True
        kind, p = task[0], task[1]
        if kind == PACK:
            pack_step(p)
        elif kind == SUM:
            group_step(p)
        elif kind == RING:
            ring_step(p, task[2], task[3], task[4])
        elif kind == END:
            end_step(p, task[2], task[3])
        elif kind == SECOND:
            second_step(p)
        elif kind == THIRD:
            third_step(p)
        else:
            last_step(p)

    square = sum(squares[1:], squares[0])
    refs["n1"][...] = square
    norm1 = [
        send(refs["n1"], refs["n1r"].at[i], refs["norm1_sem"], (i,), rel(("x", dx), ("y", dy)))
        for i, (dx, dy) in enumerate(XY_PEERS)
    ]
    rims = [
        send(state.at[:, pl.ds(64, 8), :], state.at[:, pl.ds(0, 8), :], refs["edge_sem"], (0,), flat(1)),
        send(state.at[:, pl.ds(8, 8), :], state.at[:, pl.ds(72, 8), :], refs["edge_sem"], (1,), flat(-1)),
    ]
    for copy in norm1:
        copy.wait_recv()
    for i in range(15):
        square = square + refs["n1r"][i]
    refs["n2"][...] = square
    norm2 = [
        send(refs["n2"], refs["n2r"].at[i], refs["norm2_sem"], (i,), rel(("z", dz), ("c", dc)))
        for i, (dz, dc) in enumerate(ZC_PEERS)
    ]
    count = jnp.full((8, 128), refs["step"][0].astype(F32), F32)
    first_fix = 1.0 - jnp.exp(count * math.log(0.9))
    second_fix = 1.0 - jnp.exp(count * math.log(0.95))
    early = list(started)
    for copy in early[: -len(norm2)]:
        copy.wait_send()
    for copy in rims:
        copy.wait_recv()
    for copy in norm2:
        copy.wait_recv()
    for i in range(15):
        square = square + refs["n2r"][i]
    norm = jnp.sqrt(jnp.full((8, 128), jnp.sum(square), F32))
    clip = jnp.minimum(1.0, TOTAL**0.5 / (norm + 1e-06))

    def moments(row):
        scaled = state[2, row : row + 8, :] * clip
        momentum = 0.9 * state[0, row : row + 8, :] + 0.1 * scaled
        variance = 0.95 * state[1, row : row + 8, :] + 0.05 * scaled * scaled
        return momentum, variance

    out_ref = refs["out"]
    leaving = []

    def put(src, dst):
        copy = pltpu.make_async_copy(src, dst, refs["leave_sem"].at[len(leaving)])
        copy.start()
        leaving.append(copy)

    pairs = [moments(8 * q) for q in range(10)]
    for q in range(8):
        at = slice(8 * q, 8 * q + 8)
        momentum, variance = pairs[q + 1]
        update = momentum / first_fix / (jnp.sqrt(variance / second_fix) + 1e-08)
        out_ref[1, at, :] = update
        out_ref[0, at, :] = refs["master"][at, :] * (1.0 - 0.0001 * 0.1) - 0.0001 * update
    own_rows = pl.ds(pl.multiple_of(r * ROWS, ROWS), ROWS)
    refs["half"][...] = out_ref[0].astype(BF16)
    gathers = [
        send(refs["half"], w_ref.at[own_rows, :], refs["out_sem"], (i,), in_rep(dy, dl))
        for i, (dy, dl) in enumerate(REP_PEERS)
    ]
    put(refs["half"], w_ref.at[own_rows, :])
    put(out_ref.at[0], new_hbm)
    put(out_ref.at[1], up_hbm)
    first = (o > 0).astype(F32)
    last = (o < 255).astype(F32)
    for j in range(5):
        (ma, va), (mb, vb) = pairs[2 * j], pairs[2 * j + 1]
        ma, va, mb, vb = jnp.abs(ma), jnp.abs(va), jnp.abs(mb), jnp.abs(vb)
        if j == 0:
            ma, va = ma * first, va * first
        if j == 4:
            mb, vb = mb * last, vb * last
        m_max = jnp.max(jnp.maximum(ma, mb))
        v_max = jnp.max(jnp.maximum(va, vb))
        refs["am"][j] = m_max
        refs["av"][j] = v_max
        for q in (2 * j - 1, 2 * j):
            if 0 <= q < 8:
                at = slice(8 * q, 8 * q + 8)
                out_ref[2, at, :] = pairs[q + 1][0] / (m_max + 1e-06)
                out_ref[3, at, :] = pairs[q + 1][1] / (v_max + 1e-06)
    put(out_ref.at[2], mn_hbm)
    put(out_ref.at[3], vn_hbm)
    put(refs["am"], am_hbm)
    put(refs["av"], av_hbm)
    for copy in started[len(early) - len(norm2) :]:
        copy.wait_send()
    for copy in leaving:
        copy.wait()
    for copy in gathers:
        copy.wait_recv()


def leave(*refs):
    count = 7
    sources, results, held = refs[:count], refs[count : 2 * count], refs[2 * count : 3 * count]
    sems = refs[3 * count]
    loads = [pltpu.make_async_copy(sources[i], held[i], sems.at[0, i]) for i in range(count)]
    stores = [pltpu.make_async_copy(held[i], results[i], sems.at[1, i]) for i in range(count)]
    for copy in loads:
        copy.start()
    for load, store in zip(loads, stores):
        load.wait()
        store.start()
    for copy in stores:
        copy.wait()


def on_device(grads, momentum_codes, variance_codes, momentum_scale, variance_scale, master, step):
    hbm = pl.BlockSpec(memory_space=pl.ANY)
    tile = jax.ShapeDtypeStruct((ROWS, 128), F32)
    weights = jax.ShapeDtypeStruct((16 * ROWS, 128), BF16)
    slots = jax.ShapeDtypeStruct((5,), F32)
    shapes = (tile, weights, tile, tile, tile, slots, slots)
    results = pl.pallas_call(
        kernel,
        out_shape=shapes,
        in_specs=[hbm] * 7,
        out_specs=(hbm,) * 7,
        scratch_shapes=list(layout().values()),
        compiler_params=pltpu.CompilerParams(
            collective_id=0, has_side_effects=True, vmem_limit_bytes=48 * 2**20
        ),
        name="adam_window",
    )(
        grads, momentum_codes.reshape(ROWS, 128), variance_codes.reshape(ROWS, 128),
        momentum_scale, variance_scale, master.reshape(ROWS, 128), step,
    )
    new, weights, update, m_norm, v_norm, m_max, v_max = pl.pallas_call(
        leave,
        out_shape=shapes,
        in_specs=[hbm] * 7,
        out_specs=(hbm,) * 7,
        scratch_shapes=[pltpu.VMEM(v.shape, v.dtype) for v in shapes] + [pltpu.SemaphoreType.DMA((2, 7))],
        name="leave",
    )(*results)
    return (
        new.reshape(-1), weights.reshape(-1), update.reshape(-1), m_norm.reshape(-1), v_norm.reshape(-1), m_max, v_max
    )


def solution(mesh):
    own = P(("shard", "rep"))
    return jax.shard_map(
        on_device,
        mesh=mesh,
        in_specs=(P("shard", "rep", None), own, own, own, own, own, P()),
        out_specs=(own, P("shard"), own, own, own, own, own),
        check_vma=False,
    )
```

```python
import math

import jax
import jax.numpy as jnp
from jax import lax
from jax.experimental import pallas as pl
from jax.experimental.pallas import tpu as pltpu
from jax.sharding import PartitionSpec as P

MESH = pl.DeviceIdType.MESH
F32 = jnp.float32
BF16 = jnp.bfloat16

NX, NY, NZ = 4, 4, 8
SIZES = {"x": NX, "y": NY, "z": NZ, "c": 2}
ROWS = 64
TOTAL = float(NX * NY * NZ * 2 * ROWS * 128)
GROUP = 131072
GROUP_ROWS = GROUP // 128

PARTS = (("xyz", 0, 16), ("yxz", 16, 16), ("zxy", 32, 16), ("xyz", 48, 8), ("yxz", 56, 8))

X_OFFSETS = (2, 1, 3, 0)
PLACE = {d: i for i, d in enumerate(X_OFFSETS)}


XY_PEERS = ((2, 2), (1, 2), (2, 1), (2, 3), (3, 2), (0, 2), (1, 1), (1, 3), (2, 0), (3, 1), (3, 3), (0, 1), (0, 3), (1, 0), (3, 0))
ZC_PEERS = ((4, 1), (4, 0), (3, 1), (5, 1), (3, 0), (5, 0), (2, 1), (6, 1), (2, 0), (6, 0), (1, 1), (7, 1), (1, 0), (7, 0), (0, 1))
REP_PEERS = ((2, 3), (1, 3), (2, 2), (3, 3), (0, 3), (1, 2), (2, 1), (3, 2), (0, 2), (1, 1), (2, 0), (3, 1), (0, 1), (1, 0), (3, 0))
FAR_FIRST = {4: (2, 1, 3), 8: (4, 3, 5, 2, 6, 1, 7)}


def ring_sends(n):
    order = []
    for step in range(n // 2):
        order.append((1, n // 2 - step))
        if n // 2 - 1 - step >= 1:
            order.append((0, n // 2 - 1 - step))
    return order


def half_of(d, long):
    return 1 - long if d == 0 else long


PACK, SUM, RING, END, SECOND, THIRD, LAST = range(7)
ORDER = (
    (PACK, 0), (PACK, 1), (PACK, 2), (PACK, 3), (PACK, 4), (SUM, 0), (PACK, 5), (PACK, 6), (PACK, 7), (SUM, 1),
    (RING, 0, 0, 1, 2), (RING, 0, 1, 1, 2), (RING, 3, 0, 1, 2), (RING, 3, 1, 1, 2), (SUM, 2), (SUM, 3),
    (RING, 0, 0, 0, 1), (RING, 1, 0, 1, 2), (RING, 1, 1, 0, 1), (RING, 2, 0, 1, 4), (RING, 2, 1, 0, 3),
    (RING, 3, 0, 0, 1), (RING, 4, 0, 1, 2), (RING, 4, 1, 0, 1), (SUM, 4), (SUM, 5), (RING, 0, 1, 0, 1),
    (RING, 3, 1, 0, 1), (SUM, 6), (SUM, 7), (RING, 1, 0, 0, 1), (RING, 1, 1, 1, 2), (RING, 2, 0, 0, 3),
    (RING, 2, 1, 1, 4), (RING, 4, 0, 0, 1), (RING, 4, 1, 1, 2), (RING, 0, 0, 1, 1), (RING, 0, 1, 1, 1),
    (RING, 2, 0, 1, 3), (RING, 2, 1, 0, 2), (RING, 3, 0, 1, 1), (RING, 1, 0, 1, 1), (RING, 3, 1, 1, 1),
    (END, 1, 1, 0), (RING, 4, 0, 1, 1), (END, 4, 1, 0), (RING, 2, 0, 0, 2), (RING, 2, 1, 1, 3), (END, 0, 0, 0),
    (END, 0, 1, 0), (RING, 2, 0, 1, 2), (RING, 2, 1, 0, 1), (END, 3, 0, 0), (END, 1, 0, 0), (END, 3, 1, 0),
    (RING, 1, 1, 1, 1), (RING, 2, 0, 0, 1), (RING, 2, 1, 1, 2), (END, 4, 0, 0), (RING, 4, 1, 1, 1),
    (RING, 2, 0, 1, 1), (END, 2, 1, 0), (END, 0, 0, 1), (END, 0, 1, 1), (SECOND, 0), (END, 3, 0, 1), (END, 1, 0, 1),
    (END, 3, 1, 1), (SECOND, 3), (END, 2, 0, 0), (RING, 2, 1, 1, 1), (END, 1, 1, 1), (SECOND, 1), (END, 4, 0, 1),
    (END, 2, 0, 1), (END, 4, 1, 1), (SECOND, 4), (END, 2, 1, 1), (SECOND, 2), (THIRD, 0), (THIRD, 1), (THIRD, 3),
    (THIRD, 4), (THIRD, 2), (LAST, 0), (LAST, 2), (LAST, 1), (LAST, 3), (LAST, 4),
)


def device(x, y, z, c):
    return ((x * 2 + lax.div(z, 4)) * 2 + c, y * 4 + lax.rem(z, 4))


def add_into(dst, src, rows, tile=64):
    def body(i, carry):
        at = pl.ds(pl.multiple_of(i * tile, tile), tile)
        dst[at, :] = dst[at, :] + src[at, :]
        return carry

    lax.fori_loop(0, rows // tile, body, 0)


def layout():
    dma = pltpu.SemaphoreType.DMA
    out = {
        "raw": pltpu.VMEM((1, 16 * GROUP), BF16),
        "pack": pltpu.VMEM((8, GROUP_ROWS, 128), BF16),
        "got": pltpu.VMEM((8, GROUP_ROWS, 128), BF16),
        "mcode": pltpu.VMEM((ROWS, 128), jnp.int32),
        "vcode": pltpu.VMEM((ROWS, 128), jnp.int32),
        "master": pltpu.VMEM((ROWS, 128), F32),
        "mscale": pltpu.SMEM((5,), F32),
        "vscale": pltpu.SMEM((5,), F32),
        "step": pltpu.SMEM((1,), jnp.int32),
        "state": pltpu.VMEM((3, 80, 128), F32),
        "out": pltpu.VMEM((4, ROWS, 128), F32),
        "half": pltpu.VMEM((ROWS, 128), BF16),
        "am": pltpu.SMEM((5,), F32),
        "av": pltpu.SMEM((5,), F32),
        "n1": pltpu.VMEM((8, 128), F32),
        "n2": pltpu.VMEM((8, 128), F32),
        "n1r": pltpu.VMEM((15, 8, 128), F32),
        "n2r": pltpu.VMEM((15, 8, 128), F32),
        "load_sem": dma((16,)),
        "input_sem": dma((6,)),
        "core_sem": dma((2, 8)),
        "edge_sem": dma((2, 2)),
        "norm1_sem": dma((2, 15)),
        "norm2_sem": dma((2, 15)),
        "out_sem": dma((2, 15)),
        "leave_sem": dma((7,)),
    }
    for p, (axes, _, rows) in enumerate(PARTS):
        n1, n2, n3 = (SIZES[a] for a in axes)
        out["sum", p] = pltpu.VMEM((n1, n2 * n3 * rows, 128), F32)
        out["ring", p] = pltpu.VMEM((2, n1 - 1, n2 * n3 * rows // 2, 128), F32)
        out["two", p] = pltpu.VMEM((n2 - 1, n3 * rows, 128), F32)
        out["three", p] = pltpu.VMEM((n3 - 1, rows, 128), F32)
        out["ring_sem", p] = dma((2, 2, n1 - 1))
        out["two_sem", p] = dma((2, n2 - 1))
        out["three_sem", p] = dma((2, n3 - 1))
    return out


def kernel(g_ref, mcode_ref, vcode_ref, mscale_ref, vscale_ref, master_ref, step_ref, new_hbm, w_ref, up_hbm, mn_hbm, vn_hbm, am_hbm, av_hbm, *scratches):
    refs = {}
    for name, ref in zip(layout(), scratches):
        refs[name] = ref
    raw, pack, got, state = refs["raw"], refs["pack"], refs["got"], refs["state"]
    s, r = lax.axis_index("shard"), lax.axis_index("rep")
    x, c = lax.div(s, 4), lax.rem(s, 2)
    y, zl = lax.div(r, 4), lax.rem(r, 4)
    z = lax.rem(lax.div(s, 2), 2) * 4 + zl
    here = {"x": x, "y": y, "z": z}
    o = s * 16 + r

    def rel(*moves):
        at = {"x": x, "y": y, "z": z, "c": c}
        for axis, by in moves:
            at[axis] = lax.rem(at[axis] + by + SIZES[axis], SIZES[axis])
        return device(at["x"], at["y"], at["z"], at["c"])

    def in_rep(dy, dl):
        return (s, lax.rem(y + dy, 4) * 4 + lax.rem(zl + dl, 4))

    def flat(step):
        to = lax.rem(o + step + 256, 256)
        return (lax.div(to, 16), lax.rem(to, 16))

    started = []

    def send(src, dst, sems, index, to):
        copy = pltpu.make_async_remote_copy(
            src_ref=src, dst_ref=dst, send_sem=sems.at[(0,) + index], recv_sem=sems.at[(1,) + index],
            device_id=to, device_id_type=MESH,
        )
        copy.start()
        started.append(copy)
        return copy

    barrier = pltpu.get_barrier_semaphore()
    peers = [rel(("c", 1))] + [rel((a, d)) for a in "xyz" for d in (1, -1)]
    for peer in peers:
        pl.semaphore_signal(barrier, inc=1, device_id=peer, device_id_type=MESH)

    loads = []
    for i in range(8):
        group = lax.rem(x + X_OFFSETS[i // 2], NX) * 2 + i % 2
        for own in (0, 1):
            core = c if own else 1 - c
            at = pl.multiple_of((group * 2 + core) * GROUP, GROUP)
            load = pltpu.make_async_copy(
                g_ref.at[0, :, pl.ds(at, GROUP)],
                raw.at[:, pl.ds((2 * i + own) * GROUP, GROUP)],
                refs["load_sem"].at[2 * i + own],
            )
            load.start()
            loads.append(load)
    inputs = []
    for i, (src, name) in enumerate(
        (
            (mcode_ref, "mcode"), (vcode_ref, "vcode"), (master_ref, "master"),
            (mscale_ref, "mscale"), (vscale_ref, "vscale"), (step_ref, "step"),
        )
    ):
        copy = pltpu.make_async_copy(src, refs[name], refs["input_sem"].at[i])
        copy.start()
        inputs.append(copy)

    swaps = {}

    def pack_step(i):
        loads[2 * i].wait()

        def body(k, carry):
            for u in range(4):
                at = pl.multiple_of(2 * i * GROUP + k * 8192 + u * 2048, 2048)
                pack[i, pl.ds(pl.multiple_of(k * 64 + u * 16, 16), 16), :] = raw[:, pl.ds(at, 2048)].reshape(16, 128)
            return carry

        lax.fori_loop(0, 16, body, 0)
        if i == 0:
            pl.semaphore_wait(barrier, len(peers))
        swaps[i] = send(pack.at[i], got.at[i], refs["core_sem"], (i,), rel(("c", 1)))

    def group_step(i):
        loads[2 * i + 1].wait()
        swaps[i].wait_recv()
        place = i // 2

        def body(j, carry):
            jy = lax.div(j, 4)
            jz = lax.rem(j, 4) + (i % 2) * 4
            for u in range(4):
                other = got[i, pl.ds(pl.multiple_of(j * 64 + u * 16, 16), 16), :].astype(F32)
                for v in range(2):
                    at = pl.multiple_of((2 * i + 1) * GROUP + j * 8192 + u * 2048 + v * 1024, 1024)
                    row = u * 16 + v * 8
                    both = raw[:, pl.ds(at, 1024)].astype(F32).reshape(8, 128) + other[v * 8 : v * 8 + 8]
                    for p, (axes, low, rows) in enumerate(PARTS):
                        if low <= row < low + rows:
                            first, chunk = {
                                "x": (place, jy * NZ + jz),
                                "y": (jy, place * NZ + jz),
                                "z": (jz, place * NY + jy),
                            }[axes[0]]
                            at = pl.ds(pl.multiple_of(chunk * rows + row - low, 8), 8)
                            refs["sum", p][first, at, :] = both
            return carry

        lax.fori_loop(0, 16, body, 0)

    copies = {}

    def first_index(p, distance):
        a = PARTS[p][0][0]
        n = SIZES[a]
        return PLACE[distance % n] if a == "x" else lax.rem(here[a] + distance + n, n)

    def ring_step(p, d, long, k):
        axes = PARTS[p][0]
        total, slots = refs["sum", p], refs["ring", p]
        order = ring_sends(SIZES[axes[0]])
        step = 1 - 2 * d
        half = total.shape[1] // 2
        src = total.at[first_index(p, step * k), pl.ds(half_of(d, long) * half, half), :]
        if (long, k + 1) in order:
            copies[p, d, long, k + 1].wait_recv()
            landed = slots.at[d, order.index((long, k + 1))]
            add_into(landed, src, half)
            src = landed
        event = order.index((long, k))
        copies[p, d, long, k] = send(
            src, slots.at[d, event], refs["ring_sem", p], (d, event), rel((axes[0], step))
        )

    def end_step(p, d, long):
        total, slots = refs["sum", p], refs["ring", p]
        half = total.shape[1] // 2
        copies[p, d, long, 1].wait_recv()
        event = ring_sends(SIZES[PARTS[p][0][0]]).index((long, 1))
        add_into(total.at[first_index(p, 0), pl.ds(half_of(d, long) * half, half), :], slots.at[d, event], half)

    def second_index(p, distance):
        a = PARTS[p][0][1]
        return PLACE[distance % 4] if a == "x" else lax.rem(here[a] + distance, SIZES[a])

    def second_step(p):
        axes, _, rows = PARTS[p]
        size = SIZES[axes[2]] * rows
        for d in FAR_FIRST[SIZES[axes[1]]]:
            src = refs["sum", p].at[first_index(p, 0), pl.ds(pl.multiple_of(second_index(p, d) * size, 8), size), :]
            copies["two", p, d] = send(
                src, refs["two", p].at[d - 1], refs["two_sem", p], (d - 1,), rel((axes[1], d))
            )

    def third_rows(p, distance):
        axes, _, rows = PARTS[p]
        n = SIZES[axes[2]]
        base = second_index(p, 0) * (n * rows)
        return pl.ds(pl.multiple_of(base + lax.rem(here[axes[2]] + distance, n) * rows, 8), rows)

    def third_step(p):
        axes, _, rows = PARTS[p]
        size = SIZES[axes[2]] * rows
        n = SIZES[axes[1]]
        total, slots = refs["sum", p], refs["two", p]
        for d in range(1, n):
            copies["two", p, d].wait_recv()
        first = first_index(p, 0)
        for i in range(size // 32):
            at = pl.ds(pl.multiple_of(second_index(p, 0) * size + i * 32, 8), 32)
            value = total[first, at, :]
            for d in range(1, n):
                value = value + slots[d - 1, i * 32 : i * 32 + 32, :]
            total[first, at, :] = value
        for d in FAR_FIRST[SIZES[axes[2]]]:
            copies["three", p, d] = send(
                total.at[first, third_rows(p, d), :], refs["three", p].at[d - 1], refs["three_sem", p],
                (d - 1,), rel((axes[2], d)),
            )

    squares = []

    def last_step(p):
        axes, low, rows = PARTS[p]
        value = refs["sum", p][first_index(p, 0), third_rows(p, 0), :]
        for d in range(1, SIZES[axes[2]]):
            copies["three", p, d].wait_recv()
        for d in range(1, SIZES[axes[2]]):
            value = value + refs["three", p][d - 1]
        state[2, 8 + low : 8 + low + rows, :] = value
        square = value * value
        squares.extend(square[8 * q : 8 * q + 8] for q in range(rows // 8))

    def old_step():
        for copy in inputs:
            copy.wait()
        for j in range(5):
            low, high = max(16 * j - 8, 0), min(16 * j + 8, ROWS)
            state[0, 8 + low : 8 + high, :] = refs["mcode"][low:high, :].astype(F32) / 127.0 * refs["mscale"][j]
            state[1, 8 + low : 8 + high, :] = refs["vcode"][low:high, :].astype(F32) / 255.0 * refs["vscale"][j]

    did_old = False
    for task in ORDER:
        if task[0] == SECOND and not did_old:
            old_step()
            did_old = True
        kind, p = task[0], task[1]
        if kind == PACK:
            pack_step(p)
        elif kind == SUM:
            group_step(p)
        elif kind == RING:
            ring_step(p, task[2], task[3], task[4])
        elif kind == END:
            end_step(p, task[2], task[3])
        elif kind == SECOND:
            second_step(p)
        elif kind == THIRD:
            third_step(p)
        else:
            last_step(p)

    square = sum(squares[1:], squares[0])
    refs["n1"][...] = square
    norm1 = [
        send(refs["n1"], refs["n1r"].at[i], refs["norm1_sem"], (i,), rel(("x", dx), ("y", dy)))
        for i, (dx, dy) in enumerate(XY_PEERS)
    ]
    rims = [
        send(state.at[:, pl.ds(64, 8), :], state.at[:, pl.ds(0, 8), :], refs["edge_sem"], (0,), flat(1)),
        send(state.at[:, pl.ds(8, 8), :], state.at[:, pl.ds(72, 8), :], refs["edge_sem"], (1,), flat(-1)),
    ]
    for copy in norm1:
        copy.wait_recv()
    for i in range(15):
        square = square + refs["n1r"][i]
    refs["n2"][...] = square
    norm2 = [
        send(refs["n2"], refs["n2r"].at[i], refs["norm2_sem"], (i,), rel(("z", dz), ("c", dc)))
        for i, (dz, dc) in enumerate(ZC_PEERS)
    ]
    count = jnp.full((8, 128), refs["step"][0].astype(F32), F32)
    first_fix = 1.0 - jnp.exp(count * math.log(0.9))
    second_fix = 1.0 - jnp.exp(count * math.log(0.95))
    early = list(started)
    for copy in early[: -len(norm2)]:
        copy.wait_send()
    for copy in rims:
        copy.wait_recv()
    for copy in norm2:
        copy.wait_recv()
    for i in range(15):
        square = square + refs["n2r"][i]
    norm = jnp.sqrt(jnp.full((8, 128), jnp.sum(square), F32))
    clip = jnp.minimum(1.0, TOTAL**0.5 / (norm + 1e-06))

    def moments(row):
        scaled = state[2, row : row + 8, :] * clip
        momentum = 0.9 * state[0, row : row + 8, :] + 0.1 * scaled
        variance = 0.95 * state[1, row : row + 8, :] + 0.05 * scaled * scaled
        return momentum, variance

    out_ref = refs["out"]
    leaving = []

    def put(src, dst):
        copy = pltpu.make_async_copy(src, dst, refs["leave_sem"].at[len(leaving)])
        copy.start()
        leaving.append(copy)

    pairs = [moments(8 * q) for q in range(10)]
    for q in range(8):
        at = slice(8 * q, 8 * q + 8)
        momentum, variance = pairs[q + 1]
        update = momentum / first_fix / (jnp.sqrt(variance / second_fix) + 1e-08)
        out_ref[1, at, :] = update
        out_ref[0, at, :] = refs["master"][at, :] * (1.0 - 0.0001 * 0.1) - 0.0001 * update
    own_rows = pl.ds(pl.multiple_of(r * ROWS, ROWS), ROWS)
    refs["half"][...] = out_ref[0].astype(BF16)
    gathers = [
        send(refs["half"], w_ref.at[own_rows, :], refs["out_sem"], (i,), in_rep(dy, dl))
        for i, (dy, dl) in enumerate(REP_PEERS)
    ]
    put(refs["half"], w_ref.at[own_rows, :])
    put(out_ref.at[0], new_hbm)
    put(out_ref.at[1], up_hbm)
    first = (o > 0).astype(F32)
    last = (o < 255).astype(F32)
    for j in range(5):
        (ma, va), (mb, vb) = pairs[2 * j], pairs[2 * j + 1]
        ma, va, mb, vb = jnp.abs(ma), jnp.abs(va), jnp.abs(mb), jnp.abs(vb)
        if j == 0:
            ma, va = ma * first, va * first
        if j == 4:
            mb, vb = mb * last, vb * last
        m_max = jnp.max(jnp.maximum(ma, mb))
        v_max = jnp.max(jnp.maximum(va, vb))
        refs["am"][j] = m_max
        refs["av"][j] = v_max
        for q in (2 * j - 1, 2 * j):
            if 0 <= q < 8:
                at = slice(8 * q, 8 * q + 8)
                out_ref[2, at, :] = pairs[q + 1][0] / (m_max + 1e-06)
                out_ref[3, at, :] = pairs[q + 1][1] / (v_max + 1e-06)
    put(out_ref.at[2], mn_hbm)
    put(out_ref.at[3], vn_hbm)
    put(refs["am"], am_hbm)
    put(refs["av"], av_hbm)
    for copy in started[len(early) - len(norm2) :]:
        copy.wait_send()
    for copy in leaving:
        copy.wait()
    for copy in gathers:
        copy.wait_recv()


def leave(*refs):
    count = 7
    sources, results, held = refs[:count], refs[count : 2 * count], refs[2 * count : 3 * count]
    sems = refs[3 * count]
    loads = [pltpu.make_async_copy(sources[i], held[i], sems.at[0, i]) for i in range(count)]
    stores = [pltpu.make_async_copy(held[i], results[i], sems.at[1, i]) for i in range(count)]
    for copy in loads:
        copy.start()
    for load, store in zip(loads, stores):
        load.wait()
        store.start()
    for copy in stores:
        copy.wait()


def on_device(grads, momentum_codes, variance_codes, momentum_scale, variance_scale, master, step):
    hbm = pl.BlockSpec(memory_space=pl.ANY)
    tile = jax.ShapeDtypeStruct((ROWS, 128), F32)
    weights = jax.ShapeDtypeStruct((16 * ROWS, 128), BF16)
    slots = jax.ShapeDtypeStruct((5,), F32)
    shapes = (tile, weights, tile, tile, tile, slots, slots)
    results = pl.pallas_call(
        kernel,
        out_shape=shapes,
        in_specs=[hbm] * 7,
        out_specs=(hbm,) * 7,
        scratch_shapes=list(layout().values()),
        compiler_params=pltpu.CompilerParams(
            collective_id=0, has_side_effects=True, vmem_limit_bytes=54 * 2**20
        ),
        name="adam_window",
    )(
        grads, momentum_codes.reshape(ROWS, 128), variance_codes.reshape(ROWS, 128),
        momentum_scale, variance_scale, master.reshape(ROWS, 128), step,
    )
    new, weights, update, m_norm, v_norm, m_max, v_max = pl.pallas_call(
        leave,
        out_shape=shapes,
        in_specs=[hbm] * 7,
        out_specs=(hbm,) * 7,
        scratch_shapes=[pltpu.VMEM(v.shape, v.dtype) for v in shapes] + [pltpu.SemaphoreType.DMA((2, 7))],
        compiler_params=pltpu.CompilerParams(vmem_limit_bytes=54 * 2**20),
        name="leave",
    )(*results)
    return (
        new.reshape(-1), weights.reshape(-1), update.reshape(-1), m_norm.reshape(-1), v_norm.reshape(-1), m_max, v_max
    )


def solution(mesh):
    own = P(("shard", "rep"))
    return jax.shard_map(
        on_device,
        mesh=mesh,
        in_specs=(P("shard", "rep", None), own, own, own, own, own, P()),
        out_specs=(own, P("shard"), own, own, own, own, own),
        check_vma=False,
    )
```

```python
import math

import jax
import jax.numpy as jnp
from jax import lax
from jax.experimental import pallas as pl
from jax.experimental.pallas import tpu as pltpu
from jax.sharding import PartitionSpec as P

MESH = pl.DeviceIdType.MESH
F32 = jnp.float32
BF16 = jnp.bfloat16

NX, NY, NZ = 4, 4, 8
SIZES = {"x": NX, "y": NY, "z": NZ, "c": 2}
ROWS = 64
TOTAL = float(NX * NY * NZ * 2 * ROWS * 128)
GROUP = 131072
GROUP_ROWS = GROUP // 128

PARTS = (("zxy", 0, 16), ("xyz", 16, 16), ("yxz", 32, 16), ("xyz", 48, 8), ("yxz", 56, 8))

X_OFFSETS = (2, 1, 3, 0)
PLACE = {d: i for i, d in enumerate(X_OFFSETS)}


XY_PEERS = ((2, 2), (1, 2), (2, 1), (2, 3), (3, 2), (0, 2), (1, 1), (1, 3), (2, 0), (3, 1), (3, 3), (0, 1), (0, 3), (1, 0), (3, 0))
ZC_PEERS = ((4, 1), (4, 0), (3, 1), (5, 1), (3, 0), (5, 0), (2, 1), (6, 1), (2, 0), (6, 0), (1, 1), (7, 1), (1, 0), (7, 0), (0, 1))
REP_PEERS = ((2, 3), (1, 3), (2, 2), (3, 3), (0, 3), (1, 2), (2, 1), (3, 2), (0, 2), (1, 1), (2, 0), (3, 1), (0, 1), (1, 0), (3, 0))
FAR_FIRST = {4: (2, 1, 3), 8: (4, 3, 5, 2, 6, 1, 7)}


def ring_sends(n):
    order = []
    for step in range(n // 2):
        order.append((1, n // 2 - step))
        if n // 2 - 1 - step >= 1:
            order.append((0, n // 2 - 1 - step))
    return order


def half_of(d, long):
    return 1 - long if d == 0 else long


PACK, SUM, RING, END, SECOND, THIRD, LAST = range(7)
ORDER = (
    (PACK, 0), (PACK, 1), (PACK, 2), (PACK, 3), (PACK, 4), (SUM, 0), (PACK, 5), (PACK, 6), (PACK, 7), (SUM, 1),
    (RING, 1, 0, 1, 2), (RING, 1, 1, 1, 2), (RING, 3, 0, 1, 2), (RING, 3, 1, 1, 2), (SUM, 2), (SUM, 3),
    (RING, 0, 0, 1, 4), (RING, 0, 1, 0, 3), (RING, 1, 0, 0, 1), (RING, 2, 0, 1, 2), (RING, 2, 1, 0, 1),
    (RING, 3, 0, 0, 1), (RING, 4, 0, 1, 2), (RING, 4, 1, 0, 1), (SUM, 4), (SUM, 5), (RING, 1, 1, 0, 1),
    (RING, 3, 1, 0, 1), (SUM, 6), (SUM, 7), (RING, 0, 0, 0, 3), (RING, 0, 1, 1, 4), (RING, 2, 0, 0, 1),
    (RING, 2, 1, 1, 2), (RING, 4, 0, 0, 1), (RING, 4, 1, 1, 2), (RING, 0, 0, 1, 3), (RING, 1, 0, 1, 1),
    (RING, 0, 1, 0, 2), (RING, 1, 1, 1, 1), (RING, 3, 0, 1, 1), (RING, 3, 1, 1, 1), (RING, 2, 0, 1, 1),
    (END, 2, 1, 0), (RING, 0, 0, 0, 2), (RING, 0, 1, 1, 3), (RING, 4, 0, 1, 1), (END, 4, 1, 0), (RING, 0, 0, 1, 2),
    (END, 1, 0, 0), (RING, 0, 1, 0, 1), (END, 1, 1, 0), (END, 3, 0, 0), (END, 3, 1, 0), (END, 2, 0, 0),
    (RING, 2, 1, 1, 1), (RING, 0, 0, 0, 1), (RING, 0, 1, 1, 2), (END, 4, 0, 0), (RING, 4, 1, 1, 1),
    (RING, 0, 0, 1, 1), (END, 0, 1, 0), (END, 1, 0, 1), (END, 1, 1, 1), (SECOND, 1), (END, 3, 0, 1), (END, 0, 0, 0),
    (END, 3, 1, 1), (RING, 0, 1, 1, 1), (SECOND, 3), (END, 2, 0, 1), (END, 2, 1, 1), (SECOND, 2), (END, 0, 0, 1),
    (END, 4, 0, 1), (END, 4, 1, 1), (SECOND, 4), (END, 0, 1, 1), (SECOND, 0), (THIRD, 1), (THIRD, 2), (THIRD, 3),
    (THIRD, 4), (THIRD, 0), (LAST, 1), (LAST, 0), (LAST, 2), (LAST, 3), (LAST, 4),
)


def device(x, y, z, c):
    return ((x * 2 + lax.div(z, 4)) * 2 + c, y * 4 + lax.rem(z, 4))


def add_into(dst, src, rows, tile=64):
    def body(i, carry):
        at = pl.ds(pl.multiple_of(i * tile, tile), tile)
        dst[at, :] = dst[at, :] + src[at, :]
        return carry

    lax.fori_loop(0, rows // tile, body, 0)


def layout():
    dma = pltpu.SemaphoreType.DMA
    out = {
        "raw": pltpu.VMEM((1, 16 * GROUP), BF16),
        "pack": pltpu.VMEM((8, GROUP_ROWS, 128), BF16),
        "got": pltpu.VMEM((8, GROUP_ROWS, 128), BF16),
        "mcode": pltpu.VMEM((ROWS, 128), jnp.int32),
        "vcode": pltpu.VMEM((ROWS, 128), jnp.int32),
        "master": pltpu.VMEM((ROWS, 128), F32),
        "mscale": pltpu.SMEM((5,), F32),
        "vscale": pltpu.SMEM((5,), F32),
        "step": pltpu.SMEM((1,), jnp.int32),
        "state": pltpu.VMEM((3, 80, 128), F32),
        "out": pltpu.VMEM((4, ROWS, 128), F32),
        "half": pltpu.VMEM((ROWS, 128), BF16),
        "am": pltpu.SMEM((5,), F32),
        "av": pltpu.SMEM((5,), F32),
        "n1": pltpu.VMEM((1, 128), F32),
        "n2": pltpu.VMEM((1, 128), F32),
        "n1r": pltpu.VMEM((15, 1, 128), F32),
        "n2r": pltpu.VMEM((15, 1, 128), F32),
        "load_sem": dma((16,)),
        "input_sem": dma((6,)),
        "core_sem": dma((2, 8)),
        "edge_sem": dma((2, 2)),
        "norm1_sem": dma((2, 15)),
        "norm2_sem": dma((2, 15)),
        "out_sem": dma((2, 15)),
        "leave_sem": dma((7,)),
    }
    for p, (axes, _, rows) in enumerate(PARTS):
        n1, n2, n3 = (SIZES[a] for a in axes)
        out["sum", p] = pltpu.VMEM((n1, n2 * n3 * rows, 128), F32)
        out["ring", p] = pltpu.VMEM((2, n1 - 1, n2 * n3 * rows // 2, 128), F32)
        out["two", p] = pltpu.VMEM((n2 - 1, n3 * rows, 128), F32)
        out["three", p] = pltpu.VMEM((n3 - 1, rows, 128), F32)
        out["ring_sem", p] = dma((2, 2, n1 - 1))
        out["two_sem", p] = dma((2, n2 - 1))
        out["three_sem", p] = dma((2, n3 - 1))
    return out


def kernel(g_ref, mcode_ref, vcode_ref, mscale_ref, vscale_ref, master_ref, step_ref, new_hbm, w_ref, up_hbm, mn_hbm, vn_hbm, am_hbm, av_hbm, *scratches):
    refs = {}
    for name, ref in zip(layout(), scratches):
        refs[name] = ref
    raw, pack, got, state = refs["raw"], refs["pack"], refs["got"], refs["state"]
    s, r = lax.axis_index("shard"), lax.axis_index("rep")
    x, c = lax.div(s, 4), lax.rem(s, 2)
    y, zl = lax.div(r, 4), lax.rem(r, 4)
    z = lax.rem(lax.div(s, 2), 2) * 4 + zl
    here = {"x": x, "y": y, "z": z}
    o = s * 16 + r

    def rel(*moves):
        at = {"x": x, "y": y, "z": z, "c": c}
        for axis, by in moves:
            at[axis] = lax.rem(at[axis] + by + SIZES[axis], SIZES[axis])
        return device(at["x"], at["y"], at["z"], at["c"])

    def in_rep(dy, dl):
        return (s, lax.rem(y + dy, 4) * 4 + lax.rem(zl + dl, 4))

    def flat(step):
        to = lax.rem(o + step + 256, 256)
        return (lax.div(to, 16), lax.rem(to, 16))

    started = []

    def send(src, dst, sems, index, to):
        copy = pltpu.make_async_remote_copy(
            src_ref=src, dst_ref=dst, send_sem=sems.at[(0,) + index], recv_sem=sems.at[(1,) + index],
            device_id=to, device_id_type=MESH,
        )
        copy.start()
        started.append(copy)
        return copy

    barrier = pltpu.get_barrier_semaphore()
    peers = [rel(("c", 1))] + [rel((a, d)) for a in "xyz" for d in (1, -1)]
    for peer in peers:
        pl.semaphore_signal(barrier, inc=1, device_id=peer, device_id_type=MESH)

    loads = []
    for i in range(8):
        group = lax.rem(x + X_OFFSETS[i // 2], NX) * 2 + i % 2
        for own in (0, 1):
            core = c if own else 1 - c
            at = pl.multiple_of((group * 2 + core) * GROUP, GROUP)
            load = pltpu.make_async_copy(
                g_ref.at[0, :, pl.ds(at, GROUP)],
                raw.at[:, pl.ds((2 * i + own) * GROUP, GROUP)],
                refs["load_sem"].at[2 * i + own],
            )
            load.start()
            loads.append(load)
    inputs = []

    def input_step():
        for i, (src, name) in enumerate(
            (
                (mcode_ref, "mcode"), (vcode_ref, "vcode"), (master_ref, "master"),
                (mscale_ref, "mscale"), (vscale_ref, "vscale"), (step_ref, "step"),
            )
        ):
            copy = pltpu.make_async_copy(src, refs[name], refs["input_sem"].at[i])
            copy.start()
            inputs.append(copy)

    swaps = {}

    def pack_step(i):
        loads[2 * i].wait()

        def body(k, carry):
            for u in range(4):
                at = pl.multiple_of(2 * i * GROUP + k * 8192 + u * 2048, 2048)
                pack[i, pl.ds(pl.multiple_of(k * 64 + u * 16, 16), 16), :] = raw[:, pl.ds(at, 2048)].reshape(16, 128)
            return carry

        lax.fori_loop(0, 16, body, 0)
        if i == 0:
            pl.semaphore_wait(barrier, len(peers))
        swaps[i] = send(pack.at[i], got.at[i], refs["core_sem"], (i,), rel(("c", 1)))

    def group_step(i):
        loads[2 * i + 1].wait()
        swaps[i].wait_recv()
        place = i // 2

        def body(j, carry):
            jy = lax.div(j, 4)
            jz = lax.rem(j, 4) + (i % 2) * 4
            for u in range(4):
                other = got[i, pl.ds(pl.multiple_of(j * 64 + u * 16, 16), 16), :].astype(F32)
                for v in range(2):
                    at = pl.multiple_of((2 * i + 1) * GROUP + j * 8192 + u * 2048 + v * 1024, 1024)
                    row = u * 16 + v * 8
                    both = raw[:, pl.ds(at, 1024)].astype(F32).reshape(8, 128) + other[v * 8 : v * 8 + 8]
                    for p, (axes, low, rows) in enumerate(PARTS):
                        if low <= row < low + rows:
                            first, chunk = {
                                "x": (place, jy * NZ + jz),
                                "y": (jy, place * NZ + jz),
                                "z": (jz, place * NY + jy),
                            }[axes[0]]
                            at = pl.ds(pl.multiple_of(chunk * rows + row - low, 8), 8)
                            refs["sum", p][first, at, :] = both
            return carry

        lax.fori_loop(0, 16, body, 0)

    copies = {}

    def first_index(p, distance):
        a = PARTS[p][0][0]
        n = SIZES[a]
        return PLACE[distance % n] if a == "x" else lax.rem(here[a] + distance + n, n)

    def ring_step(p, d, long, k):
        axes = PARTS[p][0]
        total, slots = refs["sum", p], refs["ring", p]
        order = ring_sends(SIZES[axes[0]])
        step = 1 - 2 * d
        half = total.shape[1] // 2
        src = total.at[first_index(p, step * k), pl.ds(half_of(d, long) * half, half), :]
        if (long, k + 1) in order:
            copies[p, d, long, k + 1].wait_recv()
            landed = slots.at[d, order.index((long, k + 1))]
            add_into(landed, src, half)
            src = landed
        event = order.index((long, k))
        copies[p, d, long, k] = send(
            src, slots.at[d, event], refs["ring_sem", p], (d, event), rel((axes[0], step))
        )

    def end_step(p, d, long):
        total, slots = refs["sum", p], refs["ring", p]
        half = total.shape[1] // 2
        copies[p, d, long, 1].wait_recv()
        event = ring_sends(SIZES[PARTS[p][0][0]]).index((long, 1))
        add_into(total.at[first_index(p, 0), pl.ds(half_of(d, long) * half, half), :], slots.at[d, event], half)

    def second_index(p, distance):
        a = PARTS[p][0][1]
        return PLACE[distance % 4] if a == "x" else lax.rem(here[a] + distance, SIZES[a])

    def second_step(p):
        axes, _, rows = PARTS[p]
        size = SIZES[axes[2]] * rows
        for d in FAR_FIRST[SIZES[axes[1]]]:
            src = refs["sum", p].at[first_index(p, 0), pl.ds(pl.multiple_of(second_index(p, d) * size, 8), size), :]
            copies["two", p, d] = send(
                src, refs["two", p].at[d - 1], refs["two_sem", p], (d - 1,), rel((axes[1], d))
            )

    def third_rows(p, distance):
        axes, _, rows = PARTS[p]
        n = SIZES[axes[2]]
        base = second_index(p, 0) * (n * rows)
        return pl.ds(pl.multiple_of(base + lax.rem(here[axes[2]] + distance, n) * rows, 8), rows)

    def third_step(p):
        axes, _, rows = PARTS[p]
        size = SIZES[axes[2]] * rows
        n = SIZES[axes[1]]
        total, slots = refs["sum", p], refs["two", p]
        for d in range(1, n):
            copies["two", p, d].wait_recv()
        first = first_index(p, 0)
        for i in range(size // 32):
            at = pl.ds(pl.multiple_of(second_index(p, 0) * size + i * 32, 8), 32)
            value = total[first, at, :]
            for d in range(1, n):
                value = value + slots[d - 1, i * 32 : i * 32 + 32, :]
            total[first, at, :] = value
        for d in FAR_FIRST[SIZES[axes[2]]]:
            copies["three", p, d] = send(
                total.at[first, third_rows(p, d), :], refs["three", p].at[d - 1], refs["three_sem", p],
                (d - 1,), rel((axes[2], d)),
            )

    squares = []

    def last_step(p):
        axes, low, rows = PARTS[p]
        value = refs["sum", p][first_index(p, 0), third_rows(p, 0), :]
        for d in range(1, SIZES[axes[2]]):
            copies["three", p, d].wait_recv()
        for d in range(1, SIZES[axes[2]]):
            value = value + refs["three", p][d - 1]
        state[2, 8 + low : 8 + low + rows, :] = value
        square = value * value
        squares.extend(square[8 * q : 8 * q + 8] for q in range(rows // 8))

    def old_step():
        for copy in inputs:
            copy.wait()
        for j in range(5):
            low, high = max(16 * j - 8, 0), min(16 * j + 8, ROWS)
            state[0, 8 + low : 8 + high, :] = refs["mcode"][low:high, :].astype(F32) / 127.0 * refs["mscale"][j]
            state[1, 8 + low : 8 + high, :] = refs["vcode"][low:high, :].astype(F32) / 255.0 * refs["vscale"][j]

    did_old = False
    for task in ORDER:
        if task[0] == SECOND and not did_old:
            old_step()
            did_old = True
        kind, p = task[0], task[1]
        if kind == PACK:
            pack_step(p)
            if p == 7:
                input_step()
        elif kind == SUM:
            group_step(p)
        elif kind == RING:
            ring_step(p, task[2], task[3], task[4])
        elif kind == END:
            end_step(p, task[2], task[3])
        elif kind == SECOND:
            second_step(p)
        elif kind == THIRD:
            third_step(p)
        else:
            last_step(p)

    square = jnp.sum(sum(squares[1:], squares[0]), axis=0, keepdims=True)
    refs["n1"][...] = square
    norm1 = [
        send(refs["n1"], refs["n1r"].at[i], refs["norm1_sem"], (i,), rel(("x", dx), ("y", dy)))
        for i, (dx, dy) in enumerate(XY_PEERS)
    ]
    rims = [
        send(state.at[:, pl.ds(64, 8), :], state.at[:, pl.ds(0, 8), :], refs["edge_sem"], (0,), flat(1)),
        send(state.at[:, pl.ds(8, 8), :], state.at[:, pl.ds(72, 8), :], refs["edge_sem"], (1,), flat(-1)),
    ]
    before = started[: -len(norm1) - len(rims)]
    part = len(before) // 3
    for copy in before[:part]:
        copy.wait_send()
    for copy in norm1:
        copy.wait_recv()
    for i in range(15):
        square = square + refs["n1r"][i]
    refs["n2"][...] = square
    norm2 = [
        send(refs["n2"], refs["n2r"].at[i], refs["norm2_sem"], (i,), rel(("z", dz), ("c", dc)))
        for i, (dz, dc) in enumerate(ZC_PEERS)
    ]
    count = jnp.full((8, 128), refs["step"][0].astype(F32), F32)
    first_fix = 1.0 - jnp.exp(count * math.log(0.9))
    second_fix = 1.0 - jnp.exp(count * math.log(0.95))
    for copy in before[part : 2 * part]:
        copy.wait_send()
    for copy in rims:
        copy.wait_recv()
    for copy in norm2:
        copy.wait_recv()
    for i in range(15):
        square = square + refs["n2r"][i]
    norm = jnp.sqrt(jnp.full((8, 128), jnp.sum(square), F32))
    clip = jnp.minimum(1.0, TOTAL**0.5 / (norm + 1e-06))

    def moments(row):
        scaled = state[2, row : row + 8, :] * clip
        momentum = 0.9 * state[0, row : row + 8, :] + 0.1 * scaled
        variance = 0.95 * state[1, row : row + 8, :] + 0.05 * scaled * scaled
        return momentum, variance

    out_ref = refs["out"]
    leaving = []

    def put(src, dst):
        copy = pltpu.make_async_copy(src, dst, refs["leave_sem"].at[len(leaving)])
        copy.start()
        leaving.append(copy)

    pairs = [moments(8 * q) for q in range(10)]
    for q in range(8):
        at = slice(8 * q, 8 * q + 8)
        momentum, variance = pairs[q + 1]
        update = momentum / first_fix / (jnp.sqrt(variance / second_fix) + 1e-08)
        out_ref[1, at, :] = update
        out_ref[0, at, :] = refs["master"][at, :] * (1.0 - 0.0001 * 0.1) - 0.0001 * update
    own_rows = pl.ds(pl.multiple_of(r * ROWS, ROWS), ROWS)
    refs["half"][...] = out_ref[0].astype(BF16)
    gathers = [
        send(refs["half"], w_ref.at[own_rows, :], refs["out_sem"], (i,), in_rep(dy, dl))
        for i, (dy, dl) in enumerate(REP_PEERS)
    ]
    put(refs["half"], w_ref.at[own_rows, :])
    put(out_ref.at[0], new_hbm)
    put(out_ref.at[1], up_hbm)
    first = (o > 0).astype(F32)
    last = (o < 255).astype(F32)
    for j in range(5):
        (ma, va), (mb, vb) = pairs[2 * j], pairs[2 * j + 1]
        ma, va, mb, vb = jnp.abs(ma), jnp.abs(va), jnp.abs(mb), jnp.abs(vb)
        if j == 0:
            ma, va = ma * first, va * first
        if j == 4:
            mb, vb = mb * last, vb * last
        m_max = jnp.max(jnp.maximum(ma, mb))
        v_max = jnp.max(jnp.maximum(va, vb))
        refs["am"][j] = m_max
        refs["av"][j] = v_max
        for q in (2 * j - 1, 2 * j):
            if 0 <= q < 8:
                at = slice(8 * q, 8 * q + 8)
                out_ref[2, at, :] = pairs[q + 1][0] / (m_max + 1e-06)
                out_ref[3, at, :] = pairs[q + 1][1] / (v_max + 1e-06)
    put(out_ref.at[2], mn_hbm)
    put(out_ref.at[3], vn_hbm)
    put(refs["am"], am_hbm)
    put(refs["av"], av_hbm)
    for copy in before[2 * part :] + norm1 + rims + norm2 + gathers:
        copy.wait_send()
    for copy in leaving:
        copy.wait()
    for copy in gathers:
        copy.wait_recv()


def leave(*refs):
    count = 7
    sources, results, held = refs[:count], refs[count : 2 * count], refs[2 * count : 3 * count]
    sems = refs[3 * count]
    loads = [pltpu.make_async_copy(sources[i], held[i], sems.at[0, i]) for i in range(count)]
    stores = [pltpu.make_async_copy(held[i], results[i], sems.at[1, i]) for i in range(count)]
    for copy in loads:
        copy.start()
    for load, store in zip(loads, stores):
        load.wait()
        store.start()
    for copy in stores:
        copy.wait()


def on_device(grads, momentum_codes, variance_codes, momentum_scale, variance_scale, master, step):
    hbm = pl.BlockSpec(memory_space=pl.ANY)
    tile = jax.ShapeDtypeStruct((ROWS, 128), F32)
    weights = jax.ShapeDtypeStruct((16 * ROWS, 128), BF16)
    slots = jax.ShapeDtypeStruct((5,), F32)
    shapes = (tile, weights, tile, tile, tile, slots, slots)
    results = pl.pallas_call(
        kernel,
        out_shape=shapes,
        in_specs=[hbm] * 7,
        out_specs=(hbm,) * 7,
        scratch_shapes=list(layout().values()),
        compiler_params=pltpu.CompilerParams(
            collective_id=0, has_side_effects=True, vmem_limit_bytes=54 * 2**20
        ),
        name="adam_window",
    )(
        grads, momentum_codes.reshape(ROWS, 128), variance_codes.reshape(ROWS, 128),
        momentum_scale, variance_scale, master.reshape(ROWS, 128), step,
    )
    new, weights, update, m_norm, v_norm, m_max, v_max = pl.pallas_call(
        leave,
        out_shape=shapes,
        in_specs=[hbm] * 7,
        out_specs=(hbm,) * 7,
        scratch_shapes=[pltpu.VMEM(v.shape, v.dtype) for v in shapes] + [pltpu.SemaphoreType.DMA((2, 7))],
        compiler_params=pltpu.CompilerParams(vmem_limit_bytes=54 * 2**20),
        name="leave",
    )(*results)
    return (
        new.reshape(-1), weights.reshape(-1), update.reshape(-1), m_norm.reshape(-1), v_norm.reshape(-1), m_max, v_max
    )


def solution(mesh):
    own = P(("shard", "rep"))
    return jax.shard_map(
        on_device,
        mesh=mesh,
        in_specs=(P("shard", "rep", None), own, own, own, own, own, P()),
        out_specs=(own, P("shard"), own, own, own, own, own),
        check_vma=False,
    )
```
